32 devices in a mesh: seq: 16 (over z, y, x), head: 2 (over core).
Axes of the slice: x: 2, y: 2, z: 4, core: 2. Of those that a mesh axis runs over, the one named last changes fastest.
Arguments:
- act: bfloat16 [8192, 4608], P('seq', 'head'), may hold values from -6 to 6
- query_rows: bfloat16 [8192, 2048], P('seq', 'head'), may hold values from -6 to 6
- key_rows: bfloat16 [8192, 1024], P('seq', 'head'), may hold values from -6 to 6
- out_adjoint: bfloat16 [8192, 2048], P('seq', 'head'), may hold values from -0.59765625 to 0.59765625
- basis_input: bfloat16 [4608, 4608], P('seq', 'head'), may hold values from -0.09375 to 0.09375
- basis_grad: bfloat16 [8, 128, 128], P('head'), may hold values from -0.5 to 0.5
- eigvals: bfloat16 [4608, 1024], P('head'), may hold values from 0.0019 to 30.5, as said below
- query_act: bfloat16 [64, 4608], P(None, 'head'), may hold values from -6 to 6
- query_adj: bfloat16 [64, 1024], P(None, 'head'), may hold values from -6 to 6
Outputs:
- influence: float32 [8192], P('seq')
The draws below stay inside these ranges and needn't reach their ends.
Inputs may be any that keep to these rules, and one draw needn't show every extreme that they name: eigvals are positive.
All inputs are finite; a program needn't handle non-finite values.
Results may differ from the reference program's by a relative error of at most 0.018.
Values may be sent and summed in bfloat16 or wider, within the bound.
A program may use at most 192 MiB of HBM per device.

```python
import math
import jax
import jax.numpy as jnp
from jax import lax

D = 4608
HD = 128
HEADS = 8
QHEADS = 16
WINDOW = 4096
LQ = 64
TOK_DEV = 512
TOKENS = 8192


def draw_eigvals(key, part):
    base_key = jax.random.fold_in(key, 11)
    row_key = jax.random.fold_in(key, 12)
    column_key = jax.random.fold_in(key, 13)
    row_scale = jnp.exp(jax.random.uniform(row_key, (D, 1), jnp.float32, 0.0, math.log(10.0)))
    rising = 1.0 + 2.0 * jnp.arange(D, dtype=jnp.float32)[:, None] / (D - 1)
    column_scale = jnp.exp(jax.random.uniform(column_key, (1, HEADS * HD), jnp.float32, 0.0, math.log(10.0)))
    base_value = jnp.exp(jax.random.uniform(base_key, (D, HEADS * HD), jnp.float32, math.log(0.05), 0.0))
    return (0.1 * base_value * row_scale * rising * column_scale).astype(jnp.bfloat16)


def block_levels(own_key, extent, pieces, least, high):
    def one(position, shards_of):
        draws = jax.random.uniform(jax.random.fold_in(jax.random.fold_in(own_key, 6), position), (shards_of,), jnp.float32, least / len(pieces), high / len(pieces))
        return jnp.repeat(jnp.exp(draws), extent[position] // shards_of).reshape((-1,) + (1,) * (len(extent) - position - 1))

    level = one(*pieces[0])
    for cut in pieces[1:]:
        level = level * one(*cut)
    return level


def gaussian(key, dims, spread, bound, cuts=(), held_as=jnp.bfloat16):
    array = jax.random.normal(key, dims, jnp.float32) * spread
    if len(cuts) > 0:
        array = block_levels(key, dims, cuts, -0.22, 0.18) * array
    return jnp.clip(array, min=-bound, max=bound).astype(held_as)


def setup_inputs(seed: int = 0) -> dict:
    key_of = jax.random.split(jax.random.key(seed), 10)
    act = gaussian(key_of[0], (TOKENS, D), 1.0, 6.0, ((0, 16), (1, 2)))
    query_rows = gaussian(key_of[1], (TOKENS, QHEADS * HD), 1.0, 6.0, ((0, 16), (1, 2)))
    key_rows = gaussian(key_of[2], (TOKENS, HEADS * HD), 1.0, 6.0, ((0, 16), (1, 2)))
    out_adjoint = gaussian(key_of[3], (TOKENS, QHEADS * HD), 0.1, 0.59765625, ((0, 16), (1, 2)))
    basis_input = gaussian(key_of[4], (D, D), D ** -0.5, 0.09375, ((0, 16), (1, 2)))
    basis_grad = gaussian(key_of[5], (HEADS, HD, HD), HD ** -0.5, 0.5, ((0, 2),))
    eigvals = draw_eigvals(jax.random.fold_in(key_of[9], 71), 0)
    query_act = gaussian(key_of[7], (LQ, D), 1.0, 6.0, ((1, 2),))
    query_adj = gaussian(key_of[8], (LQ, HEADS * HD), 1.0, 6.0, ((1, 2),))
    return {"act": act, "query_rows": query_rows, "key_rows": key_rows, "out_adjoint": out_adjoint, "basis_input": basis_input, "basis_grad": basis_grad, "eigvals": eigvals, "query_act": query_act, "query_adj": query_adj}


SCORE_SCALE = 1.0 / 12.0
SOFT_CAP = 50.0
DAMP_FACTOR = 0.1


def rotate_heads(matrix, basis_grad):
    row_count = matrix.shape[0]
    split_heads = matrix.reshape(row_count, HEADS, HD).astype(jnp.float32)
    turned = jnp.einsum("the,hef->thf", split_heads, basis_grad.astype(jnp.float32))
    return turned.reshape(row_count, HEADS * HD).astype(jnp.bfloat16)


def value_adjoints(query_rows, key_rows, out_adjoint):
    key_span = WINDOW // TOK_DEV
    block_count = TOKENS // TOK_DEV
    reach_rows = (key_span + 1) * TOK_DEV
    padded_keys = jnp.concatenate([jnp.zeros((key_span * TOK_DEV, HEADS * HD), key_rows.dtype), key_rows], axis=0)

    def one_block(carry, block):
        start = (block * TOK_DEV).astype(jnp.int32)
        queries = lax.dynamic_slice_in_dim(query_rows, start, TOK_DEV, 0).reshape(TOK_DEV, 2 * HEADS, HD).astype(jnp.float32)
        adjoint = lax.dynamic_slice_in_dim(out_adjoint, start, TOK_DEV, 0).reshape(TOK_DEV, 2 * HEADS, HD).astype(jnp.float32)
        keys_here = lax.dynamic_slice_in_dim(padded_keys, start, reach_rows, 0).reshape(reach_rows, HEADS, HD).astype(jnp.float32)
        keys_wide = jnp.repeat(keys_here, 2, axis=1)
        raw = jnp.einsum("ahd,thd->hat", queries, keys_wide) * SCORE_SCALE
        capped = SOFT_CAP * jnp.tanh(raw / SOFT_CAP)
        query_pos = start + jnp.arange(TOK_DEV, dtype=jnp.int32)
        key_pos = start - key_span * TOK_DEV + jnp.arange(reach_rows, dtype=jnp.int32)
        gap_pos = query_pos[:, None] - key_pos[None, :]
        valid = (key_pos[None, :] >= 0) & (gap_pos >= 0) & (gap_pos < WINDOW)
        weights = jnp.where(valid[None], jnp.exp(capped), jnp.zeros_like(capped))
        probs = (weights / jnp.sum(weights, axis=2, keepdims=True)).astype(jnp.bfloat16)
        partial_value = jnp.einsum("hat,ahd->thd", probs.astype(jnp.float32), adjoint)
        partial_value = jnp.sum(partial_value.reshape(reach_rows, HEADS, 2, HD), axis=2).astype(jnp.bfloat16)
        partial_value = partial_value.reshape(reach_rows, HEADS * HD).astype(jnp.float32)
        current = lax.dynamic_slice_in_dim(carry, start, reach_rows, 0)
        carry = lax.dynamic_update_slice_in_dim(carry, current + partial_value, start, 0)
        return carry, None

    initial = jnp.zeros(((block_count + key_span) * TOK_DEV, HEADS * HD), jnp.float32)
    summed, unused = lax.scan(one_block, initial, jnp.arange(block_count, dtype=jnp.int32))
    return summed[key_span * TOK_DEV:].astype(jnp.bfloat16)


def reference(act, query_rows, key_rows, out_adjoint, basis_input, basis_grad, eigvals, query_act, query_adj):
    value_adjoint = value_adjoints(query_rows, key_rows, out_adjoint)
    turned_tokens = rotate_heads(value_adjoint, basis_grad)
    turned_query = rotate_heads(query_adj, basis_grad)
    rotated_tokens = jnp.dot(act, basis_input, preferred_element_type=jnp.float32).astype(jnp.bfloat16)
    rotated_query = jnp.dot(query_act, basis_input, preferred_element_type=jnp.float32).astype(jnp.bfloat16)
    query_grad = jnp.dot(rotated_query.T, turned_query, preferred_element_type=jnp.float32) / LQ
    damping = DAMP_FACTOR * jnp.sum(eigvals.astype(jnp.float32)) / (D * HEADS * HD)
    scaled = (query_grad / (eigvals.astype(jnp.float32) + damping)).astype(jnp.bfloat16)
    mapped = jnp.dot(rotated_tokens, scaled, preferred_element_type=jnp.float32)
    return jnp.sum(mapped * turned_tokens.astype(jnp.float32), axis=1)
```

```python
import math

import jax
import jax.numpy as jnp
from jax import lax
from jax.experimental import pallas as pl
from jax.experimental.pallas import tpu as pltpu
from jax.sharding import PartitionSpec as P

WINDOW = 4096
SCORE_SCALE = 1.0 / 12.0
SOFT_CAP = 50.0
DAMP_FACTOR = 0.1
LOG2E = math.log2(math.e)


def shifted(value, by):
    size = lax.axis_size("seq")
    pairs = [(i, i + by) for i in range(size) if 0 <= i + by < size]
    return lax.ppermute(value, "seq", pairs)


def swapped(value, group, mask):
    size = lax.axis_size("seq")
    pairs = [(i, (i // group) * group + ((i % group) ^ mask)) for i in range(size)]
    return lax.ppermute(value, "seq", pairs)


def attend_kernel(key_span, place_ref, query_ref, adjoint_ref, key_ref, out_ref, weight_ref, sum_ref):
    block = pl.program_id(0)
    member = pl.program_id(1)
    depth, group, rows, width = key_ref.shape
    place = place_ref[0]
    first = place_ref[1]
    step_rows = min(rows, 256)

    @pl.when((block == 0) & (member == 0))
    def clear():
        sum_ref[...] = jnp.zeros_like(sum_ref)

    def where_is(offset):
        line = (depth - 1) * group + block - offset
        back = depth - 1 - line // group
        return back, (line % group) ^ place

    own_slot = block ^ place
    query = query_ref[own_slot]
    total_ref = weight_ref[1]
    weights = weight_ref[0]
    total_ref[...] = jnp.zeros_like(total_ref)
    for offset in range(key_span + 1):

        @pl.when(first + block >= offset)
        def score(offset=offset):
            back, slot = where_is(offset)
            for start in range(0, rows, step_rows):
                keys = key_ref[back, slot, pl.ds(start, step_rows), :]
                raw = lax.dot_general(
                    keys, query, (((1,), (1,)), ((), ())), preferred_element_type=jnp.float32
                )
                turned = jnp.tanh(raw * (SCORE_SCALE / SOFT_CAP))
                weight = jnp.exp2(turned * (SOFT_CAP * LOG2E))
                if offset == 0 or offset == key_span:
                    key_pos = start + lax.broadcasted_iota(jnp.int32, weight.shape, 0)
                    query_pos = lax.broadcasted_iota(jnp.int32, weight.shape, 1)
                    keep = key_pos <= query_pos if offset == 0 else key_pos > query_pos
                    weight = jnp.where(keep, weight, 0.0)
                total_ref[...] += jnp.sum(weight.reshape(-1, 8, rows), axis=0)
                weights[offset, pl.ds(start, step_rows), :] = weight.astype(jnp.bfloat16)

    total = jnp.sum(total_ref[...], axis=0, keepdims=True)
    inverse = jnp.broadcast_to(1.0 / total, (width, rows)).T
    scaled = (adjoint_ref[own_slot].astype(jnp.float32) * inverse).astype(jnp.bfloat16)
    for offset in range(key_span + 1):

        @pl.when(first + block >= offset)
        def spread(offset=offset):
            back, slot = where_is(offset)
            sum_ref[back, slot] += jnp.dot(
                weights[offset], scaled, preferred_element_type=jnp.float32
            )

    @pl.when((block == group - 1) & (member == 1))
    def finish():
        out_ref[...] = sum_ref[...].astype(out_ref.dtype)


def attend(place, query, adjoint, keys, key_span):
    depth, group, rows, width = keys.shape

    def body(place_ref, query_ref, adjoint_ref, key_ref, out_ref, weight_ref, total_ref, sum_ref):
        attend_kernel(
            key_span, place_ref, query_ref, adjoint_ref, key_ref, out_ref, (weight_ref, total_ref), sum_ref
        )

    tiles = 2 * group * (key_span + 1) * rows * rows
    whole = pl.BlockSpec((group, rows, width), lambda b, m: (0, 0, m))
    return pl.pallas_call(
        body,
        grid=(group, 2),
        in_specs=[
            pl.BlockSpec(memory_space=pltpu.SMEM),
            whole,
            whole,
            pl.BlockSpec((depth, group, rows, width), lambda b, m: (0, 0, 0, 0)),
        ],
        out_specs=pl.BlockSpec((depth, group, rows, width), lambda b, m: (0, 0, 0, 0)),
        out_shape=jax.ShapeDtypeStruct((depth, group, rows, width), jnp.bfloat16),
        scratch_shapes=[
            pltpu.VMEM((key_span + 1, rows, rows), jnp.bfloat16),
            pltpu.VMEM((8, rows), jnp.float32),
            pltpu.VMEM((depth, group, rows, width), jnp.float32),
        ],
        compiler_params=pltpu.CompilerParams(vmem_limit_bytes=48 * 1024 * 1024),
        cost_estimate=pl.CostEstimate(
            flops=4 * tiles * width, bytes_accessed=8 * keys.size, transcendentals=2 * tiles
        ),
    )(place, query, adjoint, keys)


def cut(value, place, width):
    return lax.dynamic_slice_in_dim(value, place * width, width, axis=1)


def on_device(
    act, query_rows, key_rows, out_adjoint, basis_input, basis_grad, eigvals, query_act, query_adj
):
    local_rows = act.shape[0]
    group = basis_grad.shape[0]
    width = basis_grad.shape[1]
    key_span = WINDOW // local_rows
    span = key_span // group
    seq_index = lax.axis_index("seq")
    place = seq_index % group

    with jax.named_scope("spread_heads"):
        key_parts, wide_parts = [], []
        for mask in range(group):
            part = cut(key_rows, place ^ mask, width)
            key_parts.append(part if mask == 0 else swapped(part, group, mask))
        for mask in range(group):
            part = jnp.concatenate(
                [
                    cut(query_rows, place ^ mask, 2 * width),
                    cut(out_adjoint, place ^ mask, 2 * width),
                ],
                axis=1,
            )
            wide_parts.append(part if mask == 0 else swapped(part, group, mask))
        own_keys = jnp.stack(key_parts)
        far_keys = [shifted(own_keys, back * group) for back in range(1, span + 1)]
        keys = jnp.stack([own_keys] + far_keys)
        wide = jnp.stack(wide_parts)

    with jax.named_scope("query_gradient"):
        row_count, column_count = basis_input.shape
        full_query_act = lax.all_gather(query_act, "head", axis=1, tiled=True)
        own_rows = lax.dynamic_slice_in_dim(
            full_query_act, seq_index * row_count, row_count, axis=1
        )
        rotated_part = jnp.dot(own_rows, basis_input, preferred_element_type=jnp.float32)
        rotated_query = lax.psum(rotated_part, "seq").astype(jnp.bfloat16)
        split_query = query_adj.reshape(query_adj.shape[0], group, width)
        turned_query = jnp.einsum(
            "the,hef->thf", split_query, basis_grad, preferred_element_type=jnp.float32
        )
        turned_query = turned_query.reshape(query_adj.shape).astype(jnp.bfloat16)
        all_turned_query = lax.all_gather(turned_query, "head", axis=1, tiled=True)
        query_grad = (
            jnp.dot(rotated_query.T, all_turned_query, preferred_element_type=jnp.float32)
            / query_act.shape[0]
        )
        eigen_total = lax.psum(jnp.sum(eigvals, dtype=jnp.float32), "head")
        damping = (
            DAMP_FACTOR * eigen_total / (eigvals.shape[0] * lax.axis_size("head") * eigvals.shape[1])
        )
        scaled = (query_grad / (eigvals.astype(jnp.float32) + damping)).astype(jnp.bfloat16)

    with jax.named_scope("token_map"):
        map_part = jnp.dot(basis_input, scaled, preferred_element_type=jnp.float32)
        map_rows = lax.psum_scatter(map_part, "head", scatter_dimension=1, tiled=True)
        token_map = lax.all_gather(map_rows.astype(jnp.bfloat16), "seq", axis=0, tiled=True)
        full_act = lax.all_gather(act, "head", axis=1, tiled=True)

    with jax.named_scope("attention"):
        spot = jnp.stack([place, seq_index - place]).astype(jnp.int32)
        partials = attend(
            spot, wide[:, :, : 2 * width], wide[:, :, 2 * width :], keys, key_span
        )
        adjoint_sum = partials[0].astype(jnp.float32)
        for back in range(1, span + 1):
            arrived = shifted(partials[back], -back * group)
            adjoint_sum = adjoint_sum + arrived.astype(jnp.float32)
        value_adjoint = adjoint_sum.astype(jnp.bfloat16)

    with jax.named_scope("gather_heads"):
        own_basis = lax.dynamic_index_in_dim(basis_grad, place, axis=0, keepdims=False)
        turned = jnp.einsum(
            "gte,ef->gtf", value_adjoint, own_basis, preferred_element_type=jnp.float32
        ).astype(jnp.bfloat16)
        parts = [turned[0]] + [swapped(turned[mask], group, mask) for mask in range(1, group)]
        stacked = jnp.stack(parts)
        turned_tokens = jnp.concatenate(
            [
                lax.dynamic_index_in_dim(stacked, place ^ head, axis=0, keepdims=False)
                for head in range(group)
            ],
            axis=1,
        )

    with jax.named_scope("influence"):
        mapped = jnp.dot(full_act, token_map, preferred_element_type=jnp.float32)
        score = jnp.sum(mapped * turned_tokens.astype(jnp.float32), axis=1)
        return lax.psum(score, "head")


def solution(mesh):
    return jax.shard_map(
        on_device,
        mesh=mesh,
        in_specs=(
            P("seq", "head"),
            P("seq", "head"),
            P("seq", "head"),
            P("seq", "head"),
            P("seq", "head"),
            P("head", None, None),
            P("head", None),
            P(None, "head"),
            P(None, "head"),
        ),
        out_specs=P("seq"),
        check_vma=False,
    )
```

```python
import math

import jax
import jax.numpy as jnp
from jax import lax
from jax.experimental import pallas as pl
from jax.experimental.pallas import tpu as pltpu
from jax.sharding import PartitionSpec as P

WINDOW = 4096
SCORE_SCALE = 1.0 / 12.0
SOFT_CAP = 50.0
DAMP_FACTOR = 0.1
LOG2E = math.log2(math.e)
MESH = pl.DeviceIdType.MESH


def shifted(value, by):
    size = lax.axis_size("seq")
    pairs = [(i, i + by) for i in range(size) if 0 <= i + by < size]
    return lax.ppermute(value, "seq", pairs)


def swapped(value, group, mask):
    size = lax.axis_size("seq")
    pairs = [(i, (i // group) * group + ((i % group) ^ mask)) for i in range(size)]
    return lax.ppermute(value, "seq", pairs)


def attend_kernel(key_span, place_ref, query_ref, adjoint_ref, key_ref, out_ref, weight_ref, sum_ref):
    block = pl.program_id(0)
    member = pl.program_id(1)
    depth, group, rows, width = key_ref.shape
    place = place_ref[0]
    first = place_ref[1]
    step_rows = min(rows, 256)

    @pl.when((block == 0) & (member == 0))
    def clear():
        sum_ref[...] = jnp.zeros_like(sum_ref)

    def where_is(offset):
        line = (depth - 1) * group + block - offset
        back = depth - 1 - line // group
        return back, (line % group) ^ place

    own_slot = block ^ place
    query = query_ref[own_slot]
    total_ref = weight_ref[1]
    weights = weight_ref[0]
    total_ref[...] = jnp.zeros_like(total_ref)
    for offset in range(key_span + 1):

        @pl.when(first + block >= offset)
        def score(offset=offset):
            back, slot = where_is(offset)
            for start in range(0, rows, step_rows):
                keys = key_ref[back, slot, pl.ds(start, step_rows), :]
                raw = lax.dot_general(
                    keys, query, (((1,), (1,)), ((), ())), preferred_element_type=jnp.float32
                )
                turned = jnp.tanh(raw * (SCORE_SCALE / SOFT_CAP))
                weight = jnp.exp2(turned * (SOFT_CAP * LOG2E))
                if offset == 0 or offset == key_span:
                    key_pos = start + lax.broadcasted_iota(jnp.int32, weight.shape, 0)
                    query_pos = lax.broadcasted_iota(jnp.int32, weight.shape, 1)
                    keep = key_pos <= query_pos if offset == 0 else key_pos > query_pos
                    weight = jnp.where(keep, weight, 0.0)
                total_ref[...] += jnp.sum(weight.reshape(-1, 8, rows), axis=0)
                weights[offset, pl.ds(start, step_rows), :] = weight.astype(jnp.bfloat16)

    total = jnp.sum(total_ref[...], axis=0, keepdims=True)
    inverse = jnp.broadcast_to(1.0 / total, (width, rows)).T
    scaled = (adjoint_ref[own_slot].astype(jnp.float32) * inverse).astype(jnp.bfloat16)
    for offset in range(key_span + 1):

        @pl.when(first + block >= offset)
        def spread(offset=offset):
            back, slot = where_is(offset)
            sum_ref[back, slot] += jnp.dot(
                weights[offset], scaled, preferred_element_type=jnp.float32
            )

    @pl.when((block == group - 1) & (member == 1))
    def finish():
        out_ref[...] = sum_ref[...].astype(out_ref.dtype)


def attend(place, query, adjoint, keys, key_span):
    depth, group, rows, width = keys.shape

    def body(place_ref, query_ref, adjoint_ref, key_ref, out_ref, weight_ref, total_ref, sum_ref):
        attend_kernel(
            key_span, place_ref, query_ref, adjoint_ref, key_ref, out_ref, (weight_ref, total_ref), sum_ref
        )

    tiles = 2 * group * (key_span + 1) * rows * rows
    whole = pl.BlockSpec((group, rows, width), lambda b, m: (0, 0, m))
    return pl.pallas_call(
        body,
        grid=(group, 2),
        in_specs=[
            pl.BlockSpec(memory_space=pltpu.SMEM),
            whole,
            whole,
            pl.BlockSpec((depth, group, rows, width), lambda b, m: (0, 0, 0, 0)),
        ],
        out_specs=pl.BlockSpec((depth, group, rows, width), lambda b, m: (0, 0, 0, 0)),
        out_shape=jax.ShapeDtypeStruct((depth, group, rows, width), jnp.bfloat16),
        scratch_shapes=[
            pltpu.VMEM((key_span + 1, rows, rows), jnp.bfloat16),
            pltpu.VMEM((8, rows), jnp.float32),
            pltpu.VMEM((depth, group, rows, width), jnp.float32),
        ],
        compiler_params=pltpu.CompilerParams(vmem_limit_bytes=48 * 1024 * 1024),
        cost_estimate=pl.CostEstimate(
            flops=4 * tiles * width, bytes_accessed=8 * keys.size, transcendentals=2 * tiles
        ),
    )(place, query, adjoint, keys)


def exchange_kernel(group, span, reduces, *refs):
    if reduces:
        part_ref, refs = refs[0], refs[1:]
    query_ref, adjoint_ref, key_ref, query_out, adjoint_out, key_out = refs[:6]
    refs = refs[6:]
    if reduces:
        rotated_out, refs = refs[0], refs[1:]
    deal_send, deal_recv, far_send, far_recv = refs[:4]
    if reduces:
        got_ref, part_send, part_recv, sum_send, sum_recv = refs[4:]
    me = lax.axis_index("seq")
    size = lax.axis_size("seq")
    place = me % group
    base = me - place
    width = key_ref.shape[1] // group

    barrier = pltpu.get_barrier_semaphore()
    for step in range(1, size):
        pl.semaphore_signal(
            barrier, inc=1, device_id={"seq": (me + step) % size}, device_id_type=MESH
        )
    pl.semaphore_wait(barrier, size - 1)

    def deal(kind, mask):
        source, target, columns = (
            (key_ref, key_out.at[0], width),
            (query_ref, query_out, 2 * width),
            (adjoint_ref, adjoint_out, 2 * width),
        )[kind]
        other = place ^ mask
        view = source.at[:, pl.ds(pl.multiple_of(other * columns, 128), columns)]
        if mask == 0:
            return pltpu.make_async_copy(view, target.at[0], deal_recv.at[kind, 0])
        return pltpu.make_async_remote_copy(
            src_ref=view,
            dst_ref=target.at[mask],
            send_sem=deal_send.at[kind, mask],
            recv_sem=deal_recv.at[kind, mask],
            device_id={"seq": base + other},
            device_id_type=MESH,
        )

    def far(back):
        return pltpu.make_async_remote_copy(
            src_ref=key_out.at[0],
            dst_ref=key_out.at[back],
            send_sem=far_send.at[back],
            recv_sem=far_recv.at[back],
            device_id={"seq": jnp.minimum(me + back * group, size - 1)},
            device_id_type=MESH,
        )

    def part(step):
        peer = (me + step) % size
        return pltpu.make_async_remote_copy(
            src_ref=part_ref.at[peer],
            dst_ref=got_ref.at[me],
            send_sem=part_send.at[step],
            recv_sem=part_recv.at[step],
            device_id={"seq": peer},
            device_id_type=MESH,
        )

    def part_arrival(step):
        peer = (me + size - step) % size
        return pltpu.make_async_remote_copy(
            src_ref=part_ref.at[me],
            dst_ref=got_ref.at[peer],
            send_sem=part_send.at[step],
            recv_sem=part_recv.at[step],
            device_id={"seq": peer},
            device_id_type=MESH,
        )

    def whole(step, source, peer):
        return pltpu.make_async_remote_copy(
            src_ref=rotated_out.at[source],
            dst_ref=rotated_out.at[source],
            send_sem=sum_send.at[step],
            recv_sem=sum_recv.at[step],
            device_id={"seq": peer},
            device_id_type=MESH,
        )

    keys = [deal(0, mask) for mask in range(group)]
    for copy in keys:
        copy.start()
    if reduces:
        parts = [part(step) for step in range(1, size)]
        for copy in parts:
            copy.start()
    wide = [deal(kind, mask) for kind in (1, 2) for mask in range(group)]
    for mask in range(group):
        for kind in (1, 2):
            wide[(kind - 1) * group + mask].start()
    keys[0].wait()
    for copy in keys[1:]:
        copy.wait_recv()
    for back in range(1, span + 1):

        @pl.when(me + back * group < size)
        def send(back=back):
            far(back).start()

    if reduces:
        got_ref[me] = part_ref[me]
        for step in range(1, size):
            part_arrival(step).wait_recv()
        total = jnp.sum(got_ref[...].astype(jnp.float32), axis=0)
        rotated_out[me] = total.astype(rotated_out.dtype)
        sums = [whole(step, me, (me + step) % size) for step in range(1, size)]
        for copy in sums:
            copy.start()
        for copy in parts:
            copy.wait_send()
        for step in range(1, size):
            whole(step, (me + size - step) % size, (me + step) % size).wait_recv()
        for copy in sums:
            copy.wait_send()

    for copy in keys[1:]:
        copy.wait_send()
    for place_in, copy in enumerate(wide):
        if place_in % group == 0:
            copy.wait()
        else:
            copy.wait_recv()
            copy.wait_send()
    for back in range(1, span + 1):

        @pl.when(me + back * group < size)
        def sent(back=back):
            far(back).wait_send()

        @pl.when(me >= back * group)
        def arrived(back=back):
            far(back).wait_recv()


def exchange(query_rows, out_adjoint, key_rows, part, group, span):
    rows, columns = key_rows.shape
    width = columns // group
    reduces = part is not None
    anywhere = pl.BlockSpec(memory_space=pl.ANY)
    in_vmem = pl.BlockSpec(memory_space=pltpu.VMEM)
    wide = jax.ShapeDtypeStruct((group, rows, 2 * width), jnp.bfloat16)
    outs = [wide, wide, jax.ShapeDtypeStruct((span + 1, group, rows, width), jnp.bfloat16)]
    specs = [anywhere] * 3
    dma = pltpu.SemaphoreType.DMA
    scratch = [dma((3, group)), dma((3, group)), dma((span + 1,)), dma((span + 1,))]
    args = (query_rows, out_adjoint, key_rows)
    in_specs = [anywhere] * 3
    if reduces:
        args = (part,) + args
        in_specs = [in_vmem] + in_specs
        outs.append(jax.ShapeDtypeStruct(part.shape, part.dtype))
        specs.append(in_vmem)
        size = part.shape[0]
        scratch = scratch + [pltpu.VMEM(part.shape, part.dtype)] + [dma((size,))] * 4

    def body(*refs):
        exchange_kernel(group, span, reduces, *refs)

    got = pl.pallas_call(
        body,
        in_specs=in_specs,
        out_specs=specs,
        out_shape=outs,
        scratch_shapes=scratch,
        compiler_params=pltpu.CompilerParams(
            collective_id=0, has_side_effects=True, vmem_limit_bytes=32 * 1024 * 1024
        ),
        cost_estimate=pl.CostEstimate(
            flops=0, bytes_accessed=16 * key_rows.size, transcendentals=0
        ),
    )(*args)
    return got if reduces else list(got) + [None]


def on_device(
    act, query_rows, key_rows, out_adjoint, basis_input, basis_grad, eigvals, query_act, query_adj
):
    local_rows = act.shape[0]
    group = basis_grad.shape[0]
    width = basis_grad.shape[1]
    key_span = WINDOW // local_rows
    span = key_span // group
    seq_index = lax.axis_index("seq")
    place = seq_index % group

    with jax.named_scope("rotated_part"):
        row_count, column_count = basis_input.shape
        query_count = query_act.shape[0]
        size = lax.axis_size("seq")
        full_query_act = lax.all_gather(query_act, "head", axis=1, tiled=True)
        own_rows = lax.dynamic_slice_in_dim(
            full_query_act, seq_index * row_count, row_count, axis=1
        )
        part = lax.dot_general(
            basis_input, own_rows, (((0,), (1,)), ((), ())), preferred_element_type=jnp.float32
        )
        reduces = column_count % (16 * size) == 0
        if reduces:
            part = part.astype(jnp.bfloat16).reshape(size, column_count // size, query_count)

    with jax.named_scope("spread_heads"):
        queries, adjoints, keys, rotated = exchange(
            query_rows, out_adjoint, key_rows, part if reduces else None, group, span
        )

    with jax.named_scope("query_gradient"):
        if reduces:
            rotated_query = rotated.reshape(column_count, query_count)
        else:
            rotated_query = lax.psum(part, "seq").astype(jnp.bfloat16)
        split_query = query_adj.reshape(query_adj.shape[0], group, width)
        turned_query = jnp.einsum(
            "the,hef->thf", split_query, basis_grad, preferred_element_type=jnp.float32
        )
        turned_query = turned_query.reshape(query_adj.shape).astype(jnp.bfloat16)
        all_turned_query = lax.all_gather(turned_query, "head", axis=1, tiled=True)
        query_grad = (
            jnp.dot(rotated_query, all_turned_query, preferred_element_type=jnp.float32)
            / query_act.shape[0]
        )
        eigen_total = lax.psum(jnp.sum(eigvals, dtype=jnp.float32), "head")
        damping = (
            DAMP_FACTOR * eigen_total / (eigvals.shape[0] * lax.axis_size("head") * eigvals.shape[1])
        )
        scaled = (query_grad / (eigvals.astype(jnp.float32) + damping)).astype(jnp.bfloat16)

    with jax.named_scope("token_map"):
        map_part = jnp.dot(basis_input, scaled, preferred_element_type=jnp.float32)
        map_rows = lax.psum_scatter(map_part, "head", scatter_dimension=1, tiled=True)
        token_map = lax.all_gather(map_rows.astype(jnp.bfloat16), "seq", axis=0, tiled=True)
        full_act = lax.all_gather(act, "head", axis=1, tiled=True)

    with jax.named_scope("attention"):
        spot = jnp.stack([place, seq_index - place]).astype(jnp.int32)
        partials = attend(
            spot, queries, adjoints, keys, key_span
        )
        adjoint_sum = partials[0].astype(jnp.float32)
        for back in range(1, span + 1):
            arrived = shifted(partials[back], -back * group)
            adjoint_sum = adjoint_sum + arrived.astype(jnp.float32)
        value_adjoint = adjoint_sum.astype(jnp.bfloat16)

    with jax.named_scope("gather_heads"):
        own_basis = lax.dynamic_index_in_dim(basis_grad, place, axis=0, keepdims=False)
        turned = jnp.einsum(
            "gte,ef->gtf", value_adjoint, own_basis, preferred_element_type=jnp.float32
        ).astype(jnp.bfloat16)
        parts = [turned[0]] + [swapped(turned[mask], group, mask) for mask in range(1, group)]
        stacked = jnp.stack(parts)
        turned_tokens = jnp.concatenate(
            [
                lax.dynamic_index_in_dim(stacked, place ^ head, axis=0, keepdims=False)
                for head in range(group)
            ],
            axis=1,
        )

    with jax.named_scope("influence"):
        mapped = jnp.dot(full_act, token_map, preferred_element_type=jnp.float32)
        score = jnp.sum(mapped * turned_tokens.astype(jnp.float32), axis=1)
        return lax.psum(score, "head")


def solution(mesh):
    return jax.shard_map(
        on_device,
        mesh=mesh,
        in_specs=(
            P("seq", "head"),
            P("seq", "head"),
            P("seq", "head"),
            P("seq", "head"),
            P("seq", "head"),
            P("head", None, None),
            P("head", None),
            P(None, "head"),
            P(None, "head"),
        ),
        out_specs=P("seq"),
        check_vma=False,
    )
```

```python
import math

import jax
import jax.numpy as jnp
from jax import lax
from jax.experimental import pallas as pl
from jax.experimental.pallas import tpu as pltpu
from jax.sharding import PartitionSpec as P

WINDOW = 4096
SCORE_SCALE = 1.0 / 12.0
SOFT_CAP = 50.0
DAMP_FACTOR = 0.1
LOG2E = math.log2(math.e)
MESH = pl.DeviceIdType.MESH


def shifted(value, by):
    size = lax.axis_size("seq")
    pairs = [(i, i + by) for i in range(size) if 0 <= i + by < size]
    return lax.ppermute(value, "seq", pairs)


def swapped(value, group, mask):
    size = lax.axis_size("seq")
    pairs = [(i, (i // group) * group + ((i % group) ^ mask)) for i in range(size)]
    return lax.ppermute(value, "seq", pairs)


def attend_kernel(key_span, query_ref, adjoint_ref, key_ref, line_ref, out_ref, map_out, scratch):
    weights, total_ref, sum_ref, spread_send, spread_recv = scratch
    block = pl.program_id(0)
    member = pl.program_id(1)
    depth, group, rows, width = key_ref.shape
    me = lax.axis_index("seq")
    place = me % group
    first = me - place
    step_rows = min(rows, 256)

    def spread_map(line, mask):
        target = map_out.at[line * group + place]
        if mask == 0:
            return pltpu.make_async_copy(line_ref.at[line], target, spread_recv.at[line, 0])
        return pltpu.make_async_remote_copy(
            src_ref=line_ref.at[line],
            dst_ref=target,
            send_sem=spread_send.at[line, mask],
            recv_sem=spread_recv.at[line, mask],
            device_id={"seq": first + (place ^ mask)},
            device_id_type=MESH,
        )

    def map_arrival(line, mask):
        return pltpu.make_async_remote_copy(
            src_ref=line_ref.at[line],
            dst_ref=map_out.at[line * group + (place ^ mask)],
            send_sem=spread_send.at[line, mask],
            recv_sem=spread_recv.at[line, mask],
            device_id={"seq": first + (place ^ mask)},
            device_id_type=MESH,
        )

    if line_ref is not None:
        lines = line_ref.shape[0]

        @pl.when((block == 0) & (member == 0))
        def start_map():
            barrier = pltpu.get_barrier_semaphore()
            for mask in range(1, group):
                pl.semaphore_signal(
                    barrier, inc=1, device_id={"seq": first + (place ^ mask)}, device_id_type=MESH
                )
            pl.semaphore_wait(barrier, group - 1)
            for line in range(lines):
                for mask in range(group):
                    spread_map(line, mask).start()

    @pl.when((block == 0) & (member == 0))
    def clear():
        sum_ref[...] = jnp.zeros_like(sum_ref)

    def where_is(offset):
        line = (depth - 1) * group + block - offset
        back = depth - 1 - line // group
        return back, (line % group) ^ place

    own_slot = block ^ place
    query = query_ref[own_slot]
    total_ref[...] = jnp.zeros_like(total_ref)
    for offset in range(key_span + 1):

        @pl.when(first + block >= offset)
        def score(offset=offset):
            back, slot = where_is(offset)
            for start in range(0, rows, step_rows):
                keys = key_ref[back, slot, pl.ds(start, step_rows), :]
                raw = lax.dot_general(
                    keys, query, (((1,), (1,)), ((), ())), preferred_element_type=jnp.float32
                )
                turned = jnp.tanh(raw * (SCORE_SCALE / SOFT_CAP))
                weight = jnp.exp2(turned * (SOFT_CAP * LOG2E))
                if offset == 0 or offset == key_span:
                    key_pos = start + lax.broadcasted_iota(jnp.int32, weight.shape, 0)
                    query_pos = lax.broadcasted_iota(jnp.int32, weight.shape, 1)
                    keep = key_pos <= query_pos if offset == 0 else key_pos > query_pos
                    weight = jnp.where(keep, weight, 0.0)
                total_ref[...] += jnp.sum(weight.reshape(-1, 8, rows), axis=0)
                weights[offset, pl.ds(start, step_rows), :] = weight.astype(jnp.bfloat16)

    total = jnp.sum(total_ref[...], axis=0, keepdims=True)
    inverse = jnp.broadcast_to(1.0 / total, (width, rows)).T
    scaled = (adjoint_ref[own_slot].astype(jnp.float32) * inverse).astype(jnp.bfloat16)
    for offset in range(key_span + 1):

        @pl.when(first + block >= offset)
        def spread(offset=offset):
            back, slot = where_is(offset)
            sum_ref[back, slot] += jnp.dot(
                weights[offset], scaled, preferred_element_type=jnp.float32
            )

    @pl.when((block == group - 1) & (member == 1))
    def finish():
        out_ref[...] = sum_ref[...].astype(out_ref.dtype)
        if line_ref is not None:
            for line in range(line_ref.shape[0]):
                spread_map(line, 0).wait()
                for mask in range(1, group):
                    map_arrival(line, mask).wait_recv()
                    spread_map(line, mask).wait_send()


def attend(query, adjoint, keys, line_map, key_span):
    depth, group, rows, width = keys.shape
    spreads = line_map is not None

    def body(*refs):
        query_ref, adjoint_ref, key_ref = refs[:3]
        if spreads:
            line_ref, out_ref, map_out = refs[3:6]
            scratch = refs[6:]
        else:
            line_ref, out_ref, map_out = None, refs[3], None
            scratch = refs[4:] + (None, None)
        attend_kernel(key_span, query_ref, adjoint_ref, key_ref, line_ref, out_ref, map_out, scratch)

    tiles = 2 * group * (key_span + 1) * rows * rows
    whole = pl.BlockSpec((group, rows, width), lambda b, m: (0, 0, m))
    every = pl.BlockSpec((depth, group, rows, width), lambda b, m: (0, 0, 0, 0))
    anywhere = pl.BlockSpec(memory_space=pl.ANY)
    args, in_specs = (query, adjoint, keys), [whole, whole, every]
    outs = [jax.ShapeDtypeStruct((depth, group, rows, width), jnp.bfloat16)]
    out_specs = [every]
    scratch = [
        pltpu.VMEM((key_span + 1, rows, rows), jnp.bfloat16),
        pltpu.VMEM((8, rows), jnp.float32),
        pltpu.VMEM((depth, group, rows, width), jnp.float32),
    ]
    params = {}
    if spreads:
        lines = line_map.shape[0]
        args, in_specs = args + (line_map,), in_specs + [anywhere]
        outs.append(jax.ShapeDtypeStruct((lines * group,) + line_map.shape[1:], line_map.dtype))
        out_specs.append(anywhere)
        scratch = scratch + [pltpu.SemaphoreType.DMA((lines, group))] * 2
        params = {"collective_id": 1, "has_side_effects": True}
    got = pl.pallas_call(
        body,
        grid=(group, 2),
        in_specs=in_specs,
        out_specs=out_specs,
        out_shape=outs,
        scratch_shapes=scratch,
        compiler_params=pltpu.CompilerParams(vmem_limit_bytes=48 * 1024 * 1024, **params),
        cost_estimate=pl.CostEstimate(
            flops=4 * tiles * width, bytes_accessed=8 * keys.size, transcendentals=2 * tiles
        ),
    )(*args)
    return got if spreads else list(got) + [None]


def exchange_kernel(group, span, reduces, *refs):
    if reduces:
        part_ref, basis_ref, eigen_ref, turned_ref = refs[:4]
        refs = refs[4:]
    query_ref, adjoint_ref, key_ref, query_out, adjoint_out, key_out = refs[:6]
    refs = refs[6:]
    if reduces:
        line_out, refs = refs[0], refs[1:]
    deal_send, deal_recv, far_send, far_recv = refs[:4]
    if reduces:
        got_ref, rotated_ref, eigen_sum, map_sum, map_got, map_rows = refs[4:10]
        part_send, part_recv, sum_send, sum_recv = refs[10:14]
        line_send, line_recv, pair_send, pair_recv = refs[14:]
    me = lax.axis_index("seq")
    size = lax.axis_size("seq")
    place = me % group
    base = me - place
    width = key_ref.shape[1] // group

    barrier = pltpu.get_barrier_semaphore()
    for step in range(1, size):
        pl.semaphore_signal(
            barrier, inc=1, device_id={"seq": (me + step) % size}, device_id_type=MESH
        )
    if reduces:
        head = lax.axis_index("head")
        pl.semaphore_signal(
            barrier, inc=1, device_id={"head": 1 - head}, device_id_type=MESH
        )
        pl.semaphore_wait(barrier, size)
    else:
        pl.semaphore_wait(barrier, size - 1)

    def deal(kind, mask):
        source, target, columns = (
            (key_ref, key_out.at[0], width),
            (query_ref, query_out, 2 * width),
            (adjoint_ref, adjoint_out, 2 * width),
        )[kind]
        other = place ^ mask
        view = source.at[:, pl.ds(pl.multiple_of(other * columns, 128), columns)]
        if mask == 0:
            return pltpu.make_async_copy(view, target.at[0], deal_recv.at[kind, 0])
        return pltpu.make_async_remote_copy(
            src_ref=view,
            dst_ref=target.at[mask],
            send_sem=deal_send.at[kind, mask],
            recv_sem=deal_recv.at[kind, mask],
            device_id={"seq": base + other},
            device_id_type=MESH,
        )

    def far(back):
        return pltpu.make_async_remote_copy(
            src_ref=key_out.at[0],
            dst_ref=key_out.at[back],
            send_sem=far_send.at[back],
            recv_sem=far_recv.at[back],
            device_id={"seq": jnp.minimum(me + back * group, size - 1)},
            device_id_type=MESH,
        )

    def part(step):
        peer = (me + step) % size
        return pltpu.make_async_remote_copy(
            src_ref=part_ref.at[peer],
            dst_ref=got_ref.at[me],
            send_sem=part_send.at[step],
            recv_sem=part_recv.at[step],
            device_id={"seq": peer},
            device_id_type=MESH,
        )

    def part_arrival(step):
        peer = (me + size - step) % size
        return pltpu.make_async_remote_copy(
            src_ref=part_ref.at[me],
            dst_ref=got_ref.at[peer],
            send_sem=part_send.at[step],
            recv_sem=part_recv.at[step],
            device_id={"seq": peer},
            device_id_type=MESH,
        )

    def whole(step, source, peer):
        depth = part_ref.shape[1]
        view = rotated_ref.at[pl.ds(pl.multiple_of(source * depth, 16), depth), :]
        return pltpu.make_async_remote_copy(
            src_ref=view,
            dst_ref=view,
            send_sem=sum_send.at[step],
            recv_sem=sum_recv.at[step],
            device_id={"seq": peer},
            device_id_type=MESH,
        )

    def pair(which, source, target):
        return pltpu.make_async_remote_copy(
            src_ref=source,
            dst_ref=target,
            send_sem=pair_send.at[which],
            recv_sem=pair_recv.at[which],
            device_id={"head": 1 - head},
            device_id_type=MESH,
        )

    lines = size // group

    def line(step, owner):
        return pltpu.make_async_remote_copy(
            src_ref=map_rows,
            dst_ref=line_out.at[owner],
            send_sem=line_send.at[step],
            recv_sem=line_recv.at[step],
            device_id={"seq": (me + step * group) % size},
            device_id_type=MESH,
        )

    keys = [deal(0, mask) for mask in range(group)]
    for copy in keys:
        copy.start()
    if reduces:
        parts = [part(step) for step in range(1, size)]
        for copy in parts:
            copy.start()
        features, outputs = eigen_ref.shape
        chunk = 256 if features % 256 == 0 else 128

        def add_eigen(index, total):
            some = eigen_ref[pl.ds(pl.multiple_of(index * chunk, chunk), chunk), :]
            return total + jnp.sum(some.astype(jnp.float32).reshape(-1, 8, outputs), axis=0)

        eigen_part = lax.fori_loop(
            0, features // chunk, add_eigen, jnp.zeros((8, outputs), jnp.float32)
        )
        eigen_part = jnp.sum(eigen_part, axis=0, keepdims=True)
        eigen_part = jnp.sum(eigen_part, axis=1, keepdims=True)
        eigen_sum[0] = jnp.broadcast_to(eigen_part, (8, 128))
        eigen_copy = pair(0, eigen_sum.at[0], eigen_sum.at[1])
        eigen_copy.start()
    keys[0].wait()
    for copy in keys[1:]:
        copy.wait_recv()
    for back in range(1, span + 1):

        @pl.when(me + back * group < size)
        def send(back=back):
            far(back).start()

    wide = [deal(kind, mask) for kind in (1, 2) for mask in range(group)]
    for mask in range(group):
        for kind in (1, 2):
            wide[(kind - 1) * group + mask].start()

    if reduces:
        got_ref[me] = part_ref[me]
        for step in range(1, size):
            part_arrival(step).wait_recv()
        total = jnp.sum(got_ref[...].astype(jnp.float32), axis=0)
        depth = part_ref.shape[1]
        rotated_ref[pl.ds(pl.multiple_of(me * depth, 16), depth), :] = total.astype(
            rotated_ref.dtype
        )
        sums = [whole(step, me, (me + step) % size) for step in range(1, size)]
        for copy in sums:
            copy.start()
        for copy in parts:
            copy.wait_send()
        for step in range(1, size):
            whole(step, (me + size - step) % size, (me + step) % size).wait_recv()
        for copy in sums:
            copy.wait_send()
        eigen_copy.wait()
        damping = (eigen_sum[0, 0:1, 0:1] + eigen_sum[1, 0:1, 0:1]) * (
            DAMP_FACTOR / (2 * features * outputs)
        )
        map_sum[...] = jnp.zeros_like(map_sum)

        def add_map(index, unused):
            start = pl.multiple_of(index * chunk, chunk)
            gradient = jnp.dot(
                rotated_ref[pl.ds(start, chunk), :],
                turned_ref[...],
                preferred_element_type=jnp.float32,
            )
            spectrum = eigen_ref[pl.ds(start, chunk), :].astype(jnp.float32) + damping
            scaled = (gradient * (1.0 / turned_ref.shape[0]) / spectrum).astype(jnp.bfloat16)
            map_sum[...] += jnp.dot(
                basis_ref[:, pl.ds(start, chunk)], scaled, preferred_element_type=jnp.float32
            )
            return unused

        lax.fori_loop(0, features // chunk, add_map, 0)
        half = outputs // 2
        own = pl.ds(pl.multiple_of(head * half, 128), half)
        other = pl.ds(pl.multiple_of((1 - head) * half, 128), half)
        map_copy = pair(1, map_sum.at[:, other], map_got)
        map_copy.start()
        map_copy.wait()
        map_rows[...] = (map_sum[:, own] + map_got[...]).astype(jnp.bfloat16)
        here = pltpu.make_async_copy(map_rows, line_out.at[me // group], line_recv.at[0])
        here.start()
        line_copies = [line(step, me // group) for step in range(1, lines)]
        for copy in line_copies:
            copy.start()
        here.wait()
        for step in range(1, lines):
            line(step, (me // group + lines - step) % lines).wait_recv()
        for copy in line_copies:
            copy.wait_send()

    for copy in keys[1:]:
        copy.wait_send()
    for place_in, copy in enumerate(wide):
        if place_in % group == 0:
            copy.wait()
        else:
            copy.wait_recv()
            copy.wait_send()
    for back in range(1, span + 1):

        @pl.when(me + back * group < size)
        def sent(back=back):
            far(back).wait_send()

        @pl.when(me >= back * group)
        def arrived(back=back):
            far(back).wait_recv()


def exchange(query_rows, out_adjoint, key_rows, map_inputs, group, span):
    rows, columns = key_rows.shape
    width = columns // group
    reduces = map_inputs is not None
    anywhere = pl.BlockSpec(memory_space=pl.ANY)
    in_vmem = pl.BlockSpec(memory_space=pltpu.VMEM)
    wide = jax.ShapeDtypeStruct((group, rows, 2 * width), jnp.bfloat16)
    outs = [wide, wide, jax.ShapeDtypeStruct((span + 1, group, rows, width), jnp.bfloat16)]
    dma = pltpu.SemaphoreType.DMA
    scratch = [dma((3, group)), dma((3, group)), dma((span + 1,)), dma((span + 1,))]
    args = (query_rows, out_adjoint, key_rows)
    in_specs = [anywhere] * 3
    flops = 0
    if reduces:
        part, basis, eigvals, turned = map_inputs
        size, depth, count = part.shape
        lines, outputs = size // group, eigvals.shape[1]
        own_map = (basis.shape[0], outputs // 2)
        args = tuple(map_inputs) + args
        in_specs = [in_vmem] * 4 + in_specs
        outs.append(jax.ShapeDtypeStruct((lines,) + own_map, jnp.bfloat16))
        scratch = scratch + [
            pltpu.VMEM(part.shape, part.dtype),
            pltpu.VMEM((size * depth, count), part.dtype),
            pltpu.VMEM((2, 8, 128), jnp.float32),
            pltpu.VMEM((basis.shape[0], outputs), jnp.float32),
            pltpu.VMEM(own_map, jnp.float32),
            pltpu.VMEM(own_map, jnp.bfloat16),
        ]
        scratch = scratch + [dma((size,))] * 4 + [dma((lines,))] * 2 + [dma((2,))] * 2
        flops = 2 * basis.size * outputs

    def body(*refs):
        exchange_kernel(group, span, reduces, *refs)

    got = pl.pallas_call(
        body,
        in_specs=in_specs,
        out_specs=[anywhere] * len(outs),
        out_shape=outs,
        scratch_shapes=scratch,
        compiler_params=pltpu.CompilerParams(
            collective_id=0, has_side_effects=True, vmem_limit_bytes=40 * 1024 * 1024
        ),
        cost_estimate=pl.CostEstimate(
            flops=flops, bytes_accessed=16 * key_rows.size, transcendentals=0
        ),
    )(*args)
    return got if reduces else list(got) + [None]


def on_device(
    act, query_rows, key_rows, out_adjoint, basis_input, basis_grad, eigvals, query_act, query_adj
):
    local_rows = act.shape[0]
    group = basis_grad.shape[0]
    width = basis_grad.shape[1]
    key_span = WINDOW // local_rows
    span = key_span // group
    seq_index = lax.axis_index("seq")
    place = seq_index % group

    with jax.named_scope("rotated_part"):
        row_count, column_count = basis_input.shape
        query_count = query_act.shape[0]
        size = lax.axis_size("seq")
        full_query_act = lax.all_gather(query_act, "head", axis=1, tiled=True)
        own_rows = lax.dynamic_slice_in_dim(
            full_query_act, seq_index * row_count, row_count, axis=1
        )
        part = lax.dot_general(
            basis_input, own_rows, (((0,), (1,)), ((), ())), preferred_element_type=jnp.float32
        )
        reduces = column_count % (16 * size) == 0 and lax.axis_size("head") == 2 and group > 1
        if reduces:
            part = part.astype(jnp.bfloat16).reshape(size, column_count // size, query_count)

    with jax.named_scope("turned_query"):
        split_query = query_adj.reshape(query_count, group, width)
        turned_query = jnp.einsum(
            "the,hef->thf", split_query, basis_grad, preferred_element_type=jnp.float32
        )
        turned_query = turned_query.reshape(query_adj.shape).astype(jnp.bfloat16)
        all_turned_query = lax.all_gather(turned_query, "head", axis=1, tiled=True)

    with jax.named_scope("spread_heads"):
        map_inputs = (part, basis_input, eigvals, all_turned_query) if reduces else None
        queries, adjoints, keys, line_map = exchange(
            query_rows, out_adjoint, key_rows, map_inputs, group, span
        )

    with jax.named_scope("attention"):
        partials, token_map = attend(queries, adjoints, keys, line_map, key_span)
        if reduces:
            token_map = token_map.reshape(row_count * size, -1)

    if not reduces:
        with jax.named_scope("token_map"):
            rotated_query = lax.psum(part, "seq").astype(jnp.bfloat16)
            query_grad = (
                jnp.dot(rotated_query, all_turned_query, preferred_element_type=jnp.float32)
                / query_count
            )
            eigen_total = lax.psum(jnp.sum(eigvals, dtype=jnp.float32), "head")
            eigen_count = eigvals.shape[0] * lax.axis_size("head") * eigvals.shape[1]
            damping = DAMP_FACTOR * eigen_total / eigen_count
            scaled = (query_grad / (eigvals.astype(jnp.float32) + damping)).astype(jnp.bfloat16)
            map_part = jnp.dot(basis_input, scaled, preferred_element_type=jnp.float32)
            map_rows = lax.psum_scatter(map_part, "head", scatter_dimension=1, tiled=True)
            token_map = lax.all_gather(map_rows.astype(jnp.bfloat16), "seq", axis=0, tiled=True)

    with jax.named_scope("value_adjoint"):
        full_act = lax.all_gather(act, "head", axis=1, tiled=True)
        adjoint_sum = partials[0].astype(jnp.float32)
        for back in range(1, span + 1):
            arrived = shifted(partials[back], -back * group)
            adjoint_sum = adjoint_sum + arrived.astype(jnp.float32)
        value_adjoint = adjoint_sum.astype(jnp.bfloat16)

    with jax.named_scope("gather_heads"):
        own_basis = lax.dynamic_index_in_dim(basis_grad, place, axis=0, keepdims=False)
        turned = jnp.einsum(
            "gte,ef->gtf", value_adjoint, own_basis, preferred_element_type=jnp.float32
        ).astype(jnp.bfloat16)
        parts = [turned[0]] + [swapped(turned[mask], group, mask) for mask in range(1, group)]
        stacked = jnp.stack(parts)
        turned_tokens = jnp.concatenate(
            [
                lax.dynamic_index_in_dim(stacked, place ^ head, axis=0, keepdims=False)
                for head in range(group)
            ],
            axis=1,
        )

    with jax.named_scope("influence"):
        mapped = jnp.dot(full_act, token_map, preferred_element_type=jnp.float32)
        mapped = lax.optimization_barrier(mapped)
        score = jnp.sum(mapped * turned_tokens.astype(jnp.float32), axis=1)
        return lax.psum(score, "head")


def solution(mesh):
    return jax.shard_map(
        on_device,
        mesh=mesh,
        in_specs=(
            P("seq", "head"),
            P("seq", "head"),
            P("seq", "head"),
            P("seq", "head"),
            P("seq", "head"),
            P("head", None, None),
            P("head", None),
            P(None, "head"),
            P(None, "head"),
        ),
        out_specs=P("seq"),
        check_vma=False,
    )
```

```python
import math

import jax
import jax.numpy as jnp
from jax import lax
from jax.experimental import pallas as pl
from jax.experimental.pallas import tpu as pltpu
from jax.sharding import PartitionSpec as P

WINDOW = 4096
SCORE_SCALE = 1.0 / 12.0
SOFT_CAP = 50.0
DAMP_FACTOR = 0.1
LOG2E = math.log2(math.e)
MESH = pl.DeviceIdType.MESH


def shifted(value, by):
    size = lax.axis_size("seq")
    pairs = [(i, i + by) for i in range(size) if 0 <= i + by < size]
    return lax.ppermute(value, "seq", pairs)


def swapped(value, group, mask):
    size = lax.axis_size("seq")
    pairs = [(i, (i // group) * group + ((i % group) ^ mask)) for i in range(size)]
    return lax.ppermute(value, "seq", pairs)


def attend_kernel(key_span, query_ref, adjoint_ref, key_ref, line_ref, out_ref, map_out, scratch):
    weights, total_ref, sum_ref, spread_send, spread_recv = scratch
    block = pl.program_id(0)
    member = pl.program_id(1)
    depth, group, rows, width = key_ref.shape
    me = lax.axis_index("seq")
    place = me % group
    first = me - place
    step_rows = min(rows, 256)

    def spread_map(line, mask):
        target = map_out.at[line * group + place]
        if mask == 0:
            return pltpu.make_async_copy(line_ref.at[line], target, spread_recv.at[line, 0])
        return pltpu.make_async_remote_copy(
            src_ref=line_ref.at[line],
            dst_ref=target,
            send_sem=spread_send.at[line, mask],
            recv_sem=spread_recv.at[line, mask],
            device_id={"seq": first + (place ^ mask)},
            device_id_type=MESH,
        )

    def map_arrival(line, mask):
        return pltpu.make_async_remote_copy(
            src_ref=line_ref.at[line],
            dst_ref=map_out.at[line * group + (place ^ mask)],
            send_sem=spread_send.at[line, mask],
            recv_sem=spread_recv.at[line, mask],
            device_id={"seq": first + (place ^ mask)},
            device_id_type=MESH,
        )

    def forward(line):
        came = 1 + line % 2
        view = map_out.at[line * group + (place ^ came)]
        return pltpu.make_async_remote_copy(
            src_ref=view,
            dst_ref=view,
            send_sem=spread_send.at[line, 3],
            recv_sem=spread_recv.at[line, 3],
            device_id={"seq": first + (place ^ (3 - came))},
            device_id_type=MESH,
        )

    if line_ref is not None:
        lines = line_ref.shape[0]

        @pl.when((block == 0) & (member == 0))
        def start_map():
            barrier = pltpu.get_barrier_semaphore()
            for mask in range(1, group):
                pl.semaphore_signal(
                    barrier, inc=1, device_id={"seq": first + (place ^ mask)}, device_id_type=MESH
                )
            pl.semaphore_wait(barrier, group - 1)
            for line in range(lines):
                for mask in range(group):
                    if mask != 3:
                        spread_map(line, mask).start()

        @pl.when((block == group // 2) & (member == 0))
        def forward_map():
            for line in range(lines if group == 4 else 0):
                map_arrival(line, 1 + line % 2).wait_recv()
                forward(line).start()

    @pl.when((block == 0) & (member == 0))
    def clear():
        sum_ref[...] = jnp.zeros_like(sum_ref)

    def where_is(offset):
        line = (depth - 1) * group + block - offset
        back = depth - 1 - line // group
        return back, (line % group) ^ place

    own_slot = block ^ place
    query = query_ref[own_slot]
    total_ref[...] = jnp.zeros_like(total_ref)
    for offset in range(key_span + 1):

        @pl.when(first + block >= offset)
        def score(offset=offset):
            back, slot = where_is(offset)
            for start in range(0, rows, step_rows):
                keys = key_ref[back, slot, pl.ds(start, step_rows), :]
                raw = lax.dot_general(
                    keys, query, (((1,), (1,)), ((), ())), preferred_element_type=jnp.float32
                )
                turned = jnp.tanh(raw * (SCORE_SCALE / SOFT_CAP))
                weight = jnp.exp2(turned * (SOFT_CAP * LOG2E))
                if offset == 0 or offset == key_span:
                    key_pos = start + lax.broadcasted_iota(jnp.int32, weight.shape, 0)
                    query_pos = lax.broadcasted_iota(jnp.int32, weight.shape, 1)
                    keep = key_pos <= query_pos if offset == 0 else key_pos > query_pos
                    weight = jnp.where(keep, weight, 0.0)
                total_ref[...] += jnp.sum(weight.reshape(-1, 8, rows), axis=0)
                weights[offset, pl.ds(start, step_rows), :] = weight.astype(jnp.bfloat16)

    total = jnp.sum(total_ref[...], axis=0, keepdims=True)
    inverse = jnp.broadcast_to(1.0 / total, (width, rows)).T
    scaled = (adjoint_ref[own_slot].astype(jnp.float32) * inverse).astype(jnp.bfloat16)
    for offset in range(key_span + 1):

        @pl.when(first + block >= offset)
        def spread(offset=offset):
            back, slot = where_is(offset)
            sum_ref[back, slot] += jnp.dot(
                weights[offset], scaled, preferred_element_type=jnp.float32
            )

    @pl.when((block == group - 1) & (member == 1))
    def finish():
        out_ref[...] = sum_ref[...].astype(out_ref.dtype)
        if line_ref is not None:
            for line in range(line_ref.shape[0]):
                spread_map(line, 0).wait()
                for mask in range(1, group):
                    if group != 4 or mask != 1 + line % 2:
                        map_arrival(line, mask).wait_recv()
                    (forward(line) if mask == 3 else spread_map(line, mask)).wait_send()


def attend(query, adjoint, keys, line_map, key_span):
    depth, group, rows, width = keys.shape
    spreads = line_map is not None

    def body(*refs):
        query_ref, adjoint_ref, key_ref = refs[:3]
        if spreads:
            line_ref, out_ref, map_out = refs[3:6]
            scratch = refs[6:]
        else:
            line_ref, out_ref, map_out = None, refs[3], None
            scratch = refs[4:] + (None, None)
        attend_kernel(key_span, query_ref, adjoint_ref, key_ref, line_ref, out_ref, map_out, scratch)

    tiles = 2 * group * (key_span + 1) * rows * rows
    whole = pl.BlockSpec((group, rows, width), lambda b, m: (0, 0, m))
    every = pl.BlockSpec((depth, group, rows, width), lambda b, m: (0, 0, 0, 0))
    anywhere = pl.BlockSpec(memory_space=pl.ANY)
    args, in_specs = (query, adjoint, keys), [whole, whole, every]
    outs = [jax.ShapeDtypeStruct((depth, group, rows, width), jnp.bfloat16)]
    out_specs = [every]
    scratch = [
        pltpu.VMEM((key_span + 1, rows, rows), jnp.bfloat16),
        pltpu.VMEM((8, rows), jnp.float32),
        pltpu.VMEM((depth, group, rows, width), jnp.float32),
    ]
    params = {}
    if spreads:
        lines = line_map.shape[0]
        args, in_specs = args + (line_map,), in_specs + [anywhere]
        outs.append(jax.ShapeDtypeStruct((lines * group,) + line_map.shape[1:], line_map.dtype))
        out_specs.append(anywhere)
        scratch = scratch + [pltpu.SemaphoreType.DMA((lines, group))] * 2
        params = {"collective_id": 1, "has_side_effects": True}
    got = pl.pallas_call(
        body,
        grid=(group, 2),
        in_specs=in_specs,
        out_specs=out_specs,
        out_shape=outs,
        scratch_shapes=scratch,
        compiler_params=pltpu.CompilerParams(vmem_limit_bytes=58 * 1024 * 1024, **params),
        cost_estimate=pl.CostEstimate(
            flops=4 * tiles * width, bytes_accessed=8 * keys.size, transcendentals=2 * tiles
        ),
    )(*args)
    return got if spreads else list(got) + [None]


def exchange_kernel(group, span, reduces, *refs):
    if reduces:
        part_ref, basis_any, eigen_any, turned_ref = refs[:4]
        refs = refs[4:]
    query_ref, adjoint_ref, key_ref, query_out, adjoint_out, key_out = refs[:6]
    refs = refs[6:]
    if reduces:
        line_out, refs = refs[0], refs[1:]
    deal_send, deal_recv, far_send, far_recv = refs[:4]
    if reduces:
        got_ref, rotated_ref, eigen_sum, map_sum, map_got, map_rows = refs[4:10]
        part_send, part_recv, sum_send, sum_recv = refs[10:14]
        line_send, line_recv, pair_send, pair_recv = refs[14:18]
        load_sem, basis_ref, eigen_ref = refs[18:]
    me = lax.axis_index("seq")
    size = lax.axis_size("seq")
    place = me % group
    base = me - place
    width = key_ref.shape[1] // group

    barrier = pltpu.get_barrier_semaphore()
    for step in range(1, size):
        pl.semaphore_signal(
            barrier, inc=1, device_id={"seq": (me + step) % size}, device_id_type=MESH
        )
    if reduces:
        head = lax.axis_index("head")
        pl.semaphore_signal(
            barrier, inc=1, device_id={"head": 1 - head}, device_id_type=MESH
        )
        pl.semaphore_wait(barrier, size)
    else:
        pl.semaphore_wait(barrier, size - 1)

    def deal(kind, mask):
        source, target, columns = (
            (key_ref, key_out.at[0], width),
            (query_ref, query_out, 2 * width),
            (adjoint_ref, adjoint_out, 2 * width),
        )[kind]
        other = place ^ mask
        view = source.at[:, pl.ds(pl.multiple_of(other * columns, 128), columns)]
        if mask == 0:
            return pltpu.make_async_copy(view, target.at[0], deal_recv.at[kind, 0])
        return pltpu.make_async_remote_copy(
            src_ref=view,
            dst_ref=target.at[mask],
            send_sem=deal_send.at[kind, mask],
            recv_sem=deal_recv.at[kind, mask],
            device_id={"seq": base + other},
            device_id_type=MESH,
        )

    def far(back):
        return pltpu.make_async_remote_copy(
            src_ref=key_out.at[0],
            dst_ref=key_out.at[back],
            send_sem=far_send.at[back],
            recv_sem=far_recv.at[back],
            device_id={"seq": jnp.minimum(me + back * group, size - 1)},
            device_id_type=MESH,
        )

    def part(step):
        peer = (me + step) % size
        return pltpu.make_async_remote_copy(
            src_ref=part_ref.at[peer],
            dst_ref=got_ref.at[me],
            send_sem=part_send.at[step],
            recv_sem=part_recv.at[step],
            device_id={"seq": peer},
            device_id_type=MESH,
        )

    def part_arrival(step):
        peer = (me + size - step) % size
        return pltpu.make_async_remote_copy(
            src_ref=part_ref.at[me],
            dst_ref=got_ref.at[peer],
            send_sem=part_send.at[step],
            recv_sem=part_recv.at[step],
            device_id={"seq": peer},
            device_id_type=MESH,
        )

    def whole(step, source, peer):
        depth = part_ref.shape[1]
        view = rotated_ref.at[pl.ds(pl.multiple_of(source * depth, 16), depth), :]
        return pltpu.make_async_remote_copy(
            src_ref=view,
            dst_ref=view,
            send_sem=sum_send.at[step],
            recv_sem=sum_recv.at[step],
            device_id={"seq": peer},
            device_id_type=MESH,
        )

    def pair(which, source, target):
        return pltpu.make_async_remote_copy(
            src_ref=source,
            dst_ref=target,
            send_sem=pair_send.at[which],
            recv_sem=pair_recv.at[which],
            device_id={"head": 1 - head},
            device_id_type=MESH,
        )

    lines = size // group

    def line(step, owner):
        return pltpu.make_async_remote_copy(
            src_ref=map_rows,
            dst_ref=line_out.at[owner],
            send_sem=line_send.at[step],
            recv_sem=line_recv.at[step],
            device_id={"seq": (me + step * group) % size},
            device_id_type=MESH,
        )

    keys = [deal(0, mask) for mask in range(group)]
    for copy in keys:
        copy.start()
    if reduces:
        parts = [part(step) for step in range(1, size)]
        for copy in parts:
            copy.start()
        features, outputs = eigen_ref.shape
        chunk = 256 if features % 256 == 0 else 128
        loads = [
            pltpu.make_async_copy(eigen_any, eigen_ref, load_sem.at[0]),
            pltpu.make_async_copy(basis_any, basis_ref, load_sem.at[1]),
        ]
        for copy in loads:
            copy.start()

        def add_eigen(index, total):
            some = eigen_ref[pl.ds(pl.multiple_of(index * chunk, chunk), chunk), :]
            return total + jnp.sum(some.astype(jnp.float32).reshape(-1, 8, outputs), axis=0)

        got_ref[me] = part_ref[me]
        for step in range(1, size):
            part_arrival(step).wait_recv()
        total = jnp.sum(got_ref[...].astype(jnp.float32), axis=0)
        depth = part_ref.shape[1]
        rotated_ref[pl.ds(pl.multiple_of(me * depth, 16), depth), :] = total.astype(
            rotated_ref.dtype
        )
        sums = [whole(step, me, (me + step) % size) for step in range(1, size)]
        for copy in sums:
            copy.start()
        for copy in parts:
            copy.wait_send()
        loads[0].wait()
        eigen_part = lax.fori_loop(
            0, features // chunk, add_eigen, jnp.zeros((8, outputs), jnp.float32)
        )
        eigen_part = jnp.sum(eigen_part, axis=0, keepdims=True)
        eigen_part = jnp.sum(eigen_part, axis=1, keepdims=True)
        eigen_sum[0] = jnp.broadcast_to(eigen_part, (8, 128))
        eigen_copy = pair(0, eigen_sum.at[0], eigen_sum.at[1])
        eigen_copy.start()
        for step in range(1, size):
            whole(step, (me + size - step) % size, (me + step) % size).wait_recv()
        for copy in sums:
            copy.wait_send()

    keys[0].wait()
    for copy in keys[1:]:
        copy.wait_recv()
    for back in range(1, span + 1):

        @pl.when(me + back * group < size)
        def send(back=back):
            far(back).start()

    wide = [deal(kind, mask) for kind in (1, 2) for mask in range(group)]
    for mask in range(group):
        for kind in (1, 2):
            wide[(kind - 1) * group + mask].start()

    if reduces:
        eigen_copy.wait()
        loads[1].wait()
        damping = (eigen_sum[0, 0:1, 0:1] + eigen_sum[1, 0:1, 0:1]) * (
            DAMP_FACTOR / (2 * features * outputs)
        )
        map_sum[...] = jnp.zeros_like(map_sum)

        def add_map(index, unused):
            start = pl.multiple_of(index * chunk, chunk)
            gradient = jnp.dot(
                rotated_ref[pl.ds(start, chunk), :],
                turned_ref[...],
                preferred_element_type=jnp.float32,
            )
            spectrum = eigen_ref[pl.ds(start, chunk), :].astype(jnp.float32) + damping
            scaled = (gradient * (1.0 / turned_ref.shape[0]) / spectrum).astype(jnp.bfloat16)
            map_sum[...] += jnp.dot(
                basis_ref[:, pl.ds(start, chunk)], scaled, preferred_element_type=jnp.float32
            )
            return unused

        lax.fori_loop(0, features // chunk, add_map, 0)
        half = outputs // 2
        own = pl.ds(pl.multiple_of(head * half, 128), half)
        other = pl.ds(pl.multiple_of((1 - head) * half, 128), half)
        map_copy = pair(1, map_sum.at[:, other], map_got)
        map_copy.start()
        map_copy.wait()
        map_rows[...] = (map_sum[:, own] + map_got[...]).astype(jnp.bfloat16)
        here = pltpu.make_async_copy(map_rows, line_out.at[me // group], line_recv.at[0])
        here.start()
        line_copies = [line(step, me // group) for step in range(1, lines)]
        for copy in line_copies:
            copy.start()
        here.wait()
        for step in range(1, lines):
            line(step, (me // group + lines - step) % lines).wait_recv()
        for copy in line_copies:
            copy.wait_send()

    for copy in keys[1:]:
        copy.wait_send()
    for place_in, copy in enumerate(wide):
        if place_in % group == 0:
            copy.wait()
        else:
            copy.wait_recv()
            copy.wait_send()
    for back in range(1, span + 1):

        @pl.when(me + back * group < size)
        def sent(back=back):
            far(back).wait_send()

        @pl.when(me >= back * group)
        def arrived(back=back):
            far(back).wait_recv()


def exchange(query_rows, out_adjoint, key_rows, map_inputs, group, span):
    rows, columns = key_rows.shape
    width = columns // group
    reduces = map_inputs is not None
    anywhere = pl.BlockSpec(memory_space=pl.ANY)
    in_vmem = pl.BlockSpec(memory_space=pltpu.VMEM)
    wide = jax.ShapeDtypeStruct((group, rows, 2 * width), jnp.bfloat16)
    outs = [wide, wide, jax.ShapeDtypeStruct((span + 1, group, rows, width), jnp.bfloat16)]
    dma = pltpu.SemaphoreType.DMA
    scratch = [dma((3, group)), dma((3, group)), dma((span + 1,)), dma((span + 1,))]
    args = (query_rows, out_adjoint, key_rows)
    in_specs = [anywhere] * 3
    flops = 0
    if reduces:
        part, basis, eigvals, turned = map_inputs
        size, depth, count = part.shape
        lines, outputs = size // group, eigvals.shape[1]
        own_map = (basis.shape[0], outputs // 2)
        args = tuple(map_inputs) + args
        in_specs = [in_vmem, anywhere, anywhere, in_vmem] + in_specs
        outs.append(jax.ShapeDtypeStruct((lines,) + own_map, jnp.bfloat16))
        scratch = scratch + [
            pltpu.VMEM(part.shape, part.dtype),
            pltpu.VMEM((size * depth, count), part.dtype),
            pltpu.VMEM((2, 8, 128), jnp.float32),
            pltpu.VMEM((basis.shape[0], outputs), jnp.float32),
            pltpu.VMEM(own_map, jnp.float32),
            pltpu.VMEM(own_map, jnp.bfloat16),
        ]
        scratch = scratch + [dma((size,))] * 4 + [dma((lines,))] * 2 + [dma((2,))] * 3
        scratch = scratch + [pltpu.VMEM(basis.shape, basis.dtype), pltpu.VMEM(eigvals.shape, eigvals.dtype)]
        flops = 2 * basis.size * outputs

    def body(*refs):
        exchange_kernel(group, span, reduces, *refs)

    got = pl.pallas_call(
        body,
        in_specs=in_specs,
        out_specs=[anywhere] * len(outs),
        out_shape=outs,
        scratch_shapes=scratch,
        compiler_params=pltpu.CompilerParams(
            collective_id=0, has_side_effects=True, vmem_limit_bytes=58 * 1024 * 1024
        ),
        cost_estimate=pl.CostEstimate(
            flops=flops, bytes_accessed=16 * key_rows.size, transcendentals=0
        ),
    )(*args)
    return got if reduces else list(got) + [None]


def on_device(
    act, query_rows, key_rows, out_adjoint, basis_input, basis_grad, eigvals, query_act, query_adj
):
    local_rows = act.shape[0]
    group = basis_grad.shape[0]
    width = basis_grad.shape[1]
    key_span = WINDOW // local_rows
    span = key_span // group
    seq_index = lax.axis_index("seq")
    place = seq_index % group

    with jax.named_scope("rotated_part"):
        row_count, column_count = basis_input.shape
        query_count = query_act.shape[0]
        size = lax.axis_size("seq")
        full_query_act = lax.all_gather(query_act, "head", axis=1, tiled=True)
        own_rows = lax.dynamic_slice_in_dim(
            full_query_act, seq_index * row_count, row_count, axis=1
        )
        part = lax.dot_general(
            basis_input, own_rows, (((0,), (1,)), ((), ())), preferred_element_type=jnp.float32
        )
        reduces = column_count % (16 * size) == 0 and lax.axis_size("head") == 2 and group in (2, 4)
        if reduces:
            part = part.astype(jnp.bfloat16).reshape(size, column_count // size, query_count)

    with jax.named_scope("turned_query"):
        split_query = query_adj.reshape(query_count, group, width)
        turned_query = jnp.einsum(
            "the,hef->thf", split_query, basis_grad, preferred_element_type=jnp.float32
        )
        turned_query = turned_query.reshape(query_adj.shape).astype(jnp.bfloat16)
        all_turned_query = lax.all_gather(turned_query, "head", axis=1, tiled=True)

    with jax.named_scope("spread_heads"):
        map_inputs = (part, basis_input, eigvals, all_turned_query) if reduces else None
        queries, adjoints, keys, line_map = exchange(
            query_rows, out_adjoint, key_rows, map_inputs, group, span
        )

    with jax.named_scope("attention"):
        partials, token_map = attend(queries, adjoints, keys, line_map, key_span)
        if reduces:
            token_map = token_map.reshape(row_count * size, -1)

    if not reduces:
        with jax.named_scope("token_map"):
            rotated_query = lax.psum(part, "seq").astype(jnp.bfloat16)
            query_grad = (
                jnp.dot(rotated_query, all_turned_query, preferred_element_type=jnp.float32)
                / query_count
            )
            eigen_total = lax.psum(jnp.sum(eigvals, dtype=jnp.float32), "head")
            eigen_count = eigvals.shape[0] * lax.axis_size("head") * eigvals.shape[1]
            damping = DAMP_FACTOR * eigen_total / eigen_count
            scaled = (query_grad / (eigvals.astype(jnp.float32) + damping)).astype(jnp.bfloat16)
            map_part = jnp.dot(basis_input, scaled, preferred_element_type=jnp.float32)
            map_rows = lax.psum_scatter(map_part, "head", scatter_dimension=1, tiled=True)
            token_map = lax.all_gather(map_rows.astype(jnp.bfloat16), "seq", axis=0, tiled=True)

    with jax.named_scope("value_adjoint"):
        full_act = lax.all_gather(act, "head", axis=1, tiled=True)
        mapped = jnp.dot(full_act, token_map, preferred_element_type=jnp.float32)
        mapped, own_partial = lax.optimization_barrier((mapped, partials[0]))
        adjoint_sum = own_partial.astype(jnp.float32)
        for back in range(1, span + 1):
            arrived = shifted(partials[back], -back * group)
            adjoint_sum = adjoint_sum + arrived.astype(jnp.float32)
        value_adjoint = adjoint_sum.astype(jnp.bfloat16)

    with jax.named_scope("gather_heads"):
        own_basis = lax.dynamic_index_in_dim(basis_grad, place, axis=0, keepdims=False)
        turned = jnp.einsum(
            "gte,ef->gtf", value_adjoint, own_basis, preferred_element_type=jnp.float32
        ).astype(jnp.bfloat16)
        parts = [turned[0]] + [swapped(turned[mask], group, mask) for mask in range(1, group)]
        stacked = jnp.stack(parts)
        turned_tokens = jnp.concatenate(
            [
                lax.dynamic_index_in_dim(stacked, place ^ head, axis=0, keepdims=False)
                for head in range(group)
            ],
            axis=1,
        )

    with jax.named_scope("influence"):
        score = jnp.sum(mapped * turned_tokens.astype(jnp.float32), axis=1)
        return lax.psum(score, "head")


def solution(mesh):
    return jax.shard_map(
        on_device,
        mesh=mesh,
        in_specs=(
            P("seq", "head"),
            P("seq", "head"),
            P("seq", "head"),
            P("seq", "head"),
            P("seq", "head"),
            P("head", None, None),
            P("head", None),
            P(None, "head"),
            P(None, "head"),
        ),
        out_specs=P("seq"),
        check_vma=False,
    )
```

```python
import math

import jax
import jax.numpy as jnp
from jax import lax
from jax.experimental import pallas as pl
from jax.experimental.pallas import tpu as pltpu
from jax.sharding import PartitionSpec as P

WINDOW = 4096
SCORE_SCALE = 1.0 / 12.0
SOFT_CAP = 50.0
DAMP_FACTOR = 0.1
LOG2E = math.log2(math.e)
MESH = pl.DeviceIdType.MESH


def shifted(value, by):
    size = lax.axis_size("seq")
    pairs = [(i, i + by) for i in range(size) if 0 <= i + by < size]
    return lax.ppermute(value, "seq", pairs)


def swapped(value, group, mask):
    size = lax.axis_size("seq")
    pairs = [(i, (i // group) * group + ((i % group) ^ mask)) for i in range(size)]
    return lax.ppermute(value, "seq", pairs)


def attend_kernel(key_span, query_ref, adjoint_ref, key_ref, rows_ref, out_ref, map_out, scratch):
    weights, total_ref, sum_ref, line_send, line_recv, spread_send, spread_recv = scratch
    block = pl.program_id(0)
    member = pl.program_id(1)
    depth, group, rows, width = key_ref.shape
    me = lax.axis_index("seq")
    place = me % group
    first = me - place
    step_rows = min(rows, 256)

    line = me // group
    turn = 2 * block + member

    def block_copy(index, seq, send_sem, recv_sem):
        view = map_out.at[index]
        return pltpu.make_async_remote_copy(
            src_ref=view,
            dst_ref=view,
            send_sem=send_sem,
            recv_sem=recv_sem,
            device_id={"seq": seq},
            device_id_type=MESH,
        )

    def along(stage, way, index):
        other = (line + (1 if way == 0 else lines - 1)) % lines
        return block_copy(
            index * group + place,
            other * group + place,
            line_send.at[way, stage],
            line_recv.at[way, stage],
        )

    def hop(stage, way):
        if way == 0:
            going, coming = line - stage, line - stage - 1
            return (going >= 0) & (line + 1 < lines), going, coming >= 0, coming
        going, coming = line + stage, line + stage + 1
        return (going < lines) & (line >= 1), going, coming < lines, coming

    def beside(owner, mask):
        return block_copy(
            owner * group + place,
            first + (place ^ mask),
            spread_send.at[owner, mask],
            spread_recv.at[owner, mask],
        )

    def arrival(owner, mask):
        return block_copy(
            owner * group + (place ^ mask),
            first + (place ^ mask),
            spread_send.at[owner, mask],
            spread_recv.at[owner, mask],
        )

    def forward(owner):
        came = 1 + owner % 2
        return block_copy(
            owner * group + (place ^ came),
            first + (place ^ (3 - came)),
            spread_send.at[owner, 3],
            spread_recv.at[owner, 3],
        )

    if rows_ref is not None:
        lines = map_out.shape[0] // group

        def start_hops(stage):
            for way in (0, 1):
                sends, going, unused, unused_too = hop(stage, way)

                @pl.when(sends)
                def start(way=way, going=going):
                    along(stage, way, going).start()

        def await_hops(stage):
            for way in (0, 1):
                unused, unused_too, receives, coming = hop(stage, way)

                @pl.when(receives)
                def wait(way=way, coming=coming):
                    along(stage, way, coming).wait_recv()

        @pl.when(turn == 0)
        def start_map():
            barrier = pltpu.get_barrier_semaphore()
            for mask in range(1, group):
                pl.semaphore_signal(
                    barrier, inc=1, device_id={"seq": first + (place ^ mask)}, device_id_type=MESH
                )
            for step in (1, lines - 1):
                pl.semaphore_signal(
                    barrier,
                    inc=1,
                    device_id={"seq": ((line + step) % lines) * group + place},
                    device_id_type=MESH,
                )
            here = pltpu.make_async_copy(rows_ref, map_out.at[me], line_recv.at[0, lines - 1])
            here.start()
            here.wait()
            pl.semaphore_wait(barrier, group + 1)
            start_hops(0)

        for stage in range(1, lines):

            @pl.when(turn == stage)
            def next_hop(stage=stage):
                await_hops(stage - 1)
                if stage < lines - 1:
                    start_hops(stage)
                else:
                    for owner in range(lines):
                        for mask in range(1, group):
                            if mask != 3:
                                beside(owner, mask).start()

        if group == 4:

            @pl.when(turn == lines + 2)
            def forward_map():
                for owner in range(lines):
                    arrival(owner, 1 + owner % 2).wait_recv()
                    forward(owner).start()

    @pl.when((block == 0) & (member == 0))
    def clear():
        sum_ref[...] = jnp.zeros_like(sum_ref)

    def where_is(offset):
        line = (depth - 1) * group + block - offset
        back = depth - 1 - line // group
        return back, (line % group) ^ place

    own_slot = block ^ place
    query = query_ref[own_slot]
    total_ref[...] = jnp.zeros_like(total_ref)
    for offset in range(key_span + 1):

        @pl.when(first + block >= offset)
        def score(offset=offset):
            back, slot = where_is(offset)
            for start in range(0, rows, step_rows):
                keys = key_ref[back, slot, pl.ds(start, step_rows), :]
                raw = lax.dot_general(
                    keys, query, (((1,), (1,)), ((), ())), preferred_element_type=jnp.float32
                )
                turned = jnp.tanh(raw * (SCORE_SCALE / SOFT_CAP))
                weight = jnp.exp2(turned * (SOFT_CAP * LOG2E))
                if offset == 0 or offset == key_span:
                    key_pos = start + lax.broadcasted_iota(jnp.int32, weight.shape, 0)
                    query_pos = lax.broadcasted_iota(jnp.int32, weight.shape, 1)
                    keep = key_pos <= query_pos if offset == 0 else key_pos > query_pos
                    weight = jnp.where(keep, weight, 0.0)
                total_ref[...] += jnp.sum(weight.reshape(-1, 8, rows), axis=0)
                weights[offset, pl.ds(start, step_rows), :] = weight.astype(jnp.bfloat16)

    total = jnp.sum(total_ref[...], axis=0, keepdims=True)
    inverse = jnp.broadcast_to(1.0 / total, (width, rows)).T
    scaled = (adjoint_ref[own_slot].astype(jnp.float32) * inverse).astype(jnp.bfloat16)
    for offset in range(key_span + 1):

        @pl.when(first + block >= offset)
        def spread(offset=offset):
            back, slot = where_is(offset)
            sum_ref[back, slot] += jnp.dot(
                weights[offset], scaled, preferred_element_type=jnp.float32
            )

    @pl.when((block == group - 1) & (member == 1))
    def finish():
        out_ref[...] = sum_ref[...].astype(out_ref.dtype)
        if rows_ref is not None:
            for stage in range(lines - 1):
                for way in (0, 1):
                    sends, going, unused, unused_too = hop(stage, way)

                    @pl.when(sends)
                    def sent(stage=stage, way=way, going=going):
                        along(stage, way, going).wait_send()

            for owner in range(lines):
                for mask in range(1, group):
                    if group != 4 or mask != 1 + owner % 2:
                        arrival(owner, mask).wait_recv()
                    (forward(owner) if mask == 3 else beside(owner, mask)).wait_send()


def attend(query, adjoint, keys, map_rows, size, key_span):
    depth, group, rows, width = keys.shape
    spreads = map_rows is not None

    def body(*refs):
        query_ref, adjoint_ref, key_ref = refs[:3]
        if spreads:
            rows_ref, out_ref, map_out = refs[3:6]
            scratch = refs[6:]
        else:
            rows_ref, out_ref, map_out = None, refs[3], None
            scratch = refs[4:] + (None,) * 4
        attend_kernel(key_span, query_ref, adjoint_ref, key_ref, rows_ref, out_ref, map_out, scratch)

    tiles = 2 * group * (key_span + 1) * rows * rows
    whole = pl.BlockSpec((group, rows, width), lambda b, m: (0, 0, m))
    every = pl.BlockSpec((depth, group, rows, width), lambda b, m: (0, 0, 0, 0))
    anywhere = pl.BlockSpec(memory_space=pl.ANY)
    args, in_specs = (query, adjoint, keys), [whole, whole, every]
    outs = [jax.ShapeDtypeStruct((depth, group, rows, width), jnp.bfloat16)]
    out_specs = [every]
    scratch = [
        pltpu.VMEM((key_span + 1, rows, rows), jnp.bfloat16),
        pltpu.VMEM((8, rows), jnp.float32),
        pltpu.VMEM((depth, group, rows, width), jnp.float32),
    ]
    params = {}
    if spreads:
        lines = size // group
        args, in_specs = args + (map_rows,), in_specs + [anywhere]
        outs.append(jax.ShapeDtypeStruct((size,) + map_rows.shape, map_rows.dtype))
        out_specs.append(anywhere)
        scratch = scratch + [pltpu.SemaphoreType.DMA((2, lines))] * 2
        scratch = scratch + [pltpu.SemaphoreType.DMA((lines, group))] * 2
        params = {"collective_id": 1, "has_side_effects": True}
    got = pl.pallas_call(
        body,
        grid=(group, 2),
        in_specs=in_specs,
        out_specs=out_specs,
        out_shape=outs,
        scratch_shapes=scratch,
        compiler_params=pltpu.CompilerParams(vmem_limit_bytes=58 * 1024 * 1024, **params),
        cost_estimate=pl.CostEstimate(
            flops=4 * tiles * width, bytes_accessed=8 * keys.size, transcendentals=2 * tiles
        ),
    )(*args)
    return got if spreads else list(got) + [None]


def exchange_kernel(group, span, reduces, *refs):
    if reduces:
        part_ref, basis_any, eigen_any, turned_ref = refs[:4]
        refs = refs[4:]
    query_ref, adjoint_ref, key_ref, query_out, adjoint_out, key_out = refs[:6]
    refs = refs[6:]
    if reduces:
        map_rows, refs = refs[0], refs[1:]
    deal_send, deal_recv, far_send, far_recv = refs[:4]
    if reduces:
        got_ref, rotated_ref, eigen_sum, map_sum, map_got = refs[4:9]
        part_send, part_recv, sum_send, sum_recv = refs[9:13]
        pair_send, pair_recv, load_sem, basis_ref, eigen_ref = refs[13:]
    me = lax.axis_index("seq")
    size = lax.axis_size("seq")
    place = me % group
    base = me - place
    width = key_ref.shape[1] // group

    barrier = pltpu.get_barrier_semaphore()
    for step in range(1, size):
        pl.semaphore_signal(
            barrier, inc=1, device_id={"seq": (me + step) % size}, device_id_type=MESH
        )
    if reduces:
        head = lax.axis_index("head")
        pl.semaphore_signal(
            barrier, inc=1, device_id={"head": 1 - head}, device_id_type=MESH
        )
        pl.semaphore_wait(barrier, size)
    else:
        pl.semaphore_wait(barrier, size - 1)

    def deal(kind, mask):
        source, target, columns = (
            (key_ref, key_out.at[0], width),
            (query_ref, query_out, 2 * width),
            (adjoint_ref, adjoint_out, 2 * width),
        )[kind]
        other = place ^ mask
        view = source.at[:, pl.ds(pl.multiple_of(other * columns, 128), columns)]
        if mask == 0:
            return pltpu.make_async_copy(view, target.at[0], deal_recv.at[kind, 0])
        return pltpu.make_async_remote_copy(
            src_ref=view,
            dst_ref=target.at[mask],
            send_sem=deal_send.at[kind, mask],
            recv_sem=deal_recv.at[kind, mask],
            device_id={"seq": base + other},
            device_id_type=MESH,
        )

    def far(back):
        return pltpu.make_async_remote_copy(
            src_ref=key_out.at[back - 1],
            dst_ref=key_out.at[back],
            send_sem=far_send.at[back],
            recv_sem=far_recv.at[back],
            device_id={"seq": (me + group) % size},
            device_id_type=MESH,
        )

    def sends(back):
        return (me + group < size) & (me >= (back - 1) * group)

    def part(step):
        peer = (me + step) % size
        return pltpu.make_async_remote_copy(
            src_ref=part_ref.at[peer],
            dst_ref=got_ref.at[me],
            send_sem=part_send.at[step],
            recv_sem=part_recv.at[step],
            device_id={"seq": peer},
            device_id_type=MESH,
        )

    def part_arrival(step):
        peer = (me + size - step) % size
        return pltpu.make_async_remote_copy(
            src_ref=part_ref.at[me],
            dst_ref=got_ref.at[peer],
            send_sem=part_send.at[step],
            recv_sem=part_recv.at[step],
            device_id={"seq": peer},
            device_id_type=MESH,
        )

    def whole(step, source, peer):
        depth = part_ref.shape[1]
        view = rotated_ref.at[pl.ds(pl.multiple_of(source * depth, 16), depth), :]
        return pltpu.make_async_remote_copy(
            src_ref=view,
            dst_ref=view,
            send_sem=sum_send.at[step],
            recv_sem=sum_recv.at[step],
            device_id={"seq": peer},
            device_id_type=MESH,
        )

    def pair(which, source, target):
        return pltpu.make_async_remote_copy(
            src_ref=source,
            dst_ref=target,
            send_sem=pair_send.at[which],
            recv_sem=pair_recv.at[which],
            device_id={"head": 1 - head},
            device_id_type=MESH,
        )

    keys = [deal(0, mask) for mask in range(group)]
    for copy in keys:
        copy.start()
    if reduces:
        parts = [part(step) for step in range(1, size)]
        for copy in parts:
            copy.start()
        features, outputs = eigen_ref.shape
        chunk = 256 if features % 256 == 0 else 128
        loads = [
            pltpu.make_async_copy(eigen_any, eigen_ref, load_sem.at[0]),
            pltpu.make_async_copy(basis_any, basis_ref, load_sem.at[1]),
        ]
        for copy in loads:
            copy.start()

        def add_eigen(index, total):
            some = eigen_ref[pl.ds(pl.multiple_of(index * chunk, chunk), chunk), :]
            return total + jnp.sum(some.astype(jnp.float32).reshape(-1, 8, outputs), axis=0)

        got_ref[me] = part_ref[me]
        for step in range(1, size):
            part_arrival(step).wait_recv()
        total = jnp.sum(got_ref[...].astype(jnp.float32), axis=0)
        depth = part_ref.shape[1]
        rotated_ref[pl.ds(pl.multiple_of(me * depth, 16), depth), :] = total.astype(
            rotated_ref.dtype
        )
        sums = [whole(step, me, (me + step) % size) for step in range(1, size)]
        for copy in sums:
            copy.start()
        for copy in parts:
            copy.wait_send()
        loads[0].wait()
        eigen_part = lax.fori_loop(
            0, features // chunk, add_eigen, jnp.zeros((8, outputs), jnp.float32)
        )
        eigen_part = jnp.sum(eigen_part, axis=0, keepdims=True)
        eigen_part = jnp.sum(eigen_part, axis=1, keepdims=True)
        eigen_sum[0] = jnp.broadcast_to(eigen_part, (8, 128))
        eigen_copy = pair(0, eigen_sum.at[0], eigen_sum.at[1])
        eigen_copy.start()
        for step in range(1, size):
            whole(step, (me + size - step) % size, (me + step) % size).wait_recv()
        for copy in sums:
            copy.wait_send()

    keys[0].wait()
    for copy in keys[1:]:
        copy.wait_recv()
    @pl.when(sends(1))
    def send():
        far(1).start()

    wide = [deal(kind, mask) for kind in (1, 2) for mask in range(group)]
    for mask in range(group):
        for kind in (1, 2):
            wide[(kind - 1) * group + mask].start()

    if reduces:
        eigen_copy.wait()
        loads[1].wait()
        damping = (eigen_sum[0, 0:1, 0:1] + eigen_sum[1, 0:1, 0:1]) * (
            DAMP_FACTOR / (2 * features * outputs)
        )
        map_sum[...] = jnp.zeros_like(map_sum)

        def add_map(index, unused):
            start = pl.multiple_of(index * chunk, chunk)
            gradient = jnp.dot(
                rotated_ref[pl.ds(start, chunk), :],
                turned_ref[...],
                preferred_element_type=jnp.float32,
            )
            spectrum = eigen_ref[pl.ds(start, chunk), :].astype(jnp.float32) + damping
            scaled = (gradient * (1.0 / turned_ref.shape[0]) / spectrum).astype(jnp.bfloat16)
            map_sum[...] += jnp.dot(
                basis_ref[:, pl.ds(start, chunk)], scaled, preferred_element_type=jnp.float32
            )
            return unused

        lax.fori_loop(0, features // chunk, add_map, 0)
        half = outputs // 2
        own = pl.ds(pl.multiple_of(head * half, 128), half)
        other = pl.ds(pl.multiple_of((1 - head) * half, 128), half)
        map_copy = pair(1, map_sum.at[:, other], map_got)
        map_copy.start()
        map_copy.wait()
        map_rows[...] = (map_sum[:, own] + map_got[...]).astype(jnp.bfloat16)

    for back in range(1, span + 1):

        @pl.when(me >= back * group)
        def arrived(back=back):
            far(back).wait_recv()

        if back < span:

            @pl.when(sends(back + 1))
            def pass_on(back=back):
                far(back + 1).start()

    for back in range(1, span + 1):

        @pl.when(sends(back))
        def sent(back=back):
            far(back).wait_send()

    for copy in keys[1:]:
        copy.wait_send()
    for place_in, copy in enumerate(wide):
        if place_in % group == 0:
            copy.wait()
        else:
            copy.wait_recv()
            copy.wait_send()


def exchange(query_rows, out_adjoint, key_rows, map_inputs, group, span):
    rows, columns = key_rows.shape
    width = columns // group
    reduces = map_inputs is not None
    anywhere = pl.BlockSpec(memory_space=pl.ANY)
    in_vmem = pl.BlockSpec(memory_space=pltpu.VMEM)
    wide = jax.ShapeDtypeStruct((group, rows, 2 * width), jnp.bfloat16)
    outs = [wide, wide, jax.ShapeDtypeStruct((span + 1, group, rows, width), jnp.bfloat16)]
    dma = pltpu.SemaphoreType.DMA
    scratch = [dma((3, group)), dma((3, group)), dma((span + 1,)), dma((span + 1,))]
    args = (query_rows, out_adjoint, key_rows)
    in_specs = [anywhere] * 3
    flops = 0
    if reduces:
        part, basis, eigvals, turned = map_inputs
        size, depth, count = part.shape
        outputs = eigvals.shape[1]
        own_map = (basis.shape[0], outputs // 2)
        args = tuple(map_inputs) + args
        in_specs = [in_vmem, anywhere, anywhere, in_vmem] + in_specs
        outs.append(jax.ShapeDtypeStruct(own_map, jnp.bfloat16))
        scratch = scratch + [
            pltpu.VMEM(part.shape, part.dtype),
            pltpu.VMEM((size * depth, count), part.dtype),
            pltpu.VMEM((2, 8, 128), jnp.float32),
            pltpu.VMEM((basis.shape[0], outputs), jnp.float32),
            pltpu.VMEM(own_map, jnp.float32),
        ]
        scratch = scratch + [dma((size,))] * 4 + [dma((2,))] * 3
        scratch = scratch + [pltpu.VMEM(basis.shape, basis.dtype), pltpu.VMEM(eigvals.shape, eigvals.dtype)]
        flops = 2 * basis.size * outputs

    def body(*refs):
        exchange_kernel(group, span, reduces, *refs)

    got = pl.pallas_call(
        body,
        in_specs=in_specs,
        out_specs=[anywhere] * 3 + [in_vmem] * (len(outs) - 3),
        out_shape=outs,
        scratch_shapes=scratch,
        compiler_params=pltpu.CompilerParams(
            collective_id=0, has_side_effects=True, vmem_limit_bytes=58 * 1024 * 1024
        ),
        cost_estimate=pl.CostEstimate(
            flops=flops, bytes_accessed=16 * key_rows.size, transcendentals=0
        ),
    )(*args)
    return got if reduces else list(got) + [None]


def on_device(
    act, query_rows, key_rows, out_adjoint, basis_input, basis_grad, eigvals, query_act, query_adj
):
    local_rows = act.shape[0]
    group = basis_grad.shape[0]
    width = basis_grad.shape[1]
    key_span = WINDOW // local_rows
    span = key_span // group
    seq_index = lax.axis_index("seq")
    place = seq_index % group

    with jax.named_scope("rotated_part"):
        row_count, column_count = basis_input.shape
        query_count = query_act.shape[0]
        size = lax.axis_size("seq")
        full_query_act = lax.all_gather(query_act, "head", axis=1, tiled=True)
        own_rows = lax.dynamic_slice_in_dim(
            full_query_act, seq_index * row_count, row_count, axis=1
        )
        part = lax.dot_general(
            basis_input, own_rows, (((0,), (1,)), ((), ())), preferred_element_type=jnp.float32
        )
        reduces = column_count % (16 * size) == 0 and lax.axis_size("head") == 2 and group in (2, 4)
        reduces = reduces and size // group + 2 < 2 * group
        if reduces:
            part = part.astype(jnp.bfloat16).reshape(size, column_count // size, query_count)

    with jax.named_scope("turned_query"):
        split_query = query_adj.reshape(query_count, group, width)
        turned_query = jnp.einsum(
            "the,hef->thf", split_query, basis_grad, preferred_element_type=jnp.float32
        )
        turned_query = turned_query.reshape(query_adj.shape).astype(jnp.bfloat16)
        all_turned_query = lax.all_gather(turned_query, "head", axis=1, tiled=True)

    with jax.named_scope("spread_heads"):
        map_inputs = (part, basis_input, eigvals, all_turned_query) if reduces else None
        queries, adjoints, keys, map_rows = exchange(
            query_rows, out_adjoint, key_rows, map_inputs, group, span
        )

    with jax.named_scope("attention"):
        partials, token_map = attend(queries, adjoints, keys, map_rows, size, key_span)
        if reduces:
            token_map = token_map.reshape(row_count * size, -1)

    if not reduces:
        with jax.named_scope("token_map"):
            rotated_query = lax.psum(part, "seq").astype(jnp.bfloat16)
            query_grad = (
                jnp.dot(rotated_query, all_turned_query, preferred_element_type=jnp.float32)
                / query_count
            )
            eigen_total = lax.psum(jnp.sum(eigvals, dtype=jnp.float32), "head")
            eigen_count = eigvals.shape[0] * lax.axis_size("head") * eigvals.shape[1]
            damping = DAMP_FACTOR * eigen_total / eigen_count
            scaled = (query_grad / (eigvals.astype(jnp.float32) + damping)).astype(jnp.bfloat16)
            map_part = jnp.dot(basis_input, scaled, preferred_element_type=jnp.float32)
            map_rows = lax.psum_scatter(map_part, "head", scatter_dimension=1, tiled=True)
            token_map = lax.all_gather(map_rows.astype(jnp.bfloat16), "seq", axis=0, tiled=True)

    with jax.named_scope("value_adjoint"):
        full_act = lax.all_gather(act, "head", axis=1, tiled=True)
        mapped = jnp.dot(full_act, token_map, preferred_element_type=jnp.float32)
        mapped, own_partial = lax.optimization_barrier((mapped, partials[0]))
        carried = shifted(partials[span], -group)
        for back in range(span - 1, 0, -1):
            passed = partials[back].astype(jnp.float32) + carried.astype(jnp.float32)
            carried = shifted(passed.astype(jnp.bfloat16), -group)
        adjoint_sum = own_partial.astype(jnp.float32) + carried.astype(jnp.float32)
        value_adjoint = adjoint_sum.astype(jnp.bfloat16)

    with jax.named_scope("gather_heads"):
        own_basis = lax.dynamic_index_in_dim(basis_grad, place, axis=0, keepdims=False)
        turned = jnp.einsum(
            "gte,ef->gtf", value_adjoint, own_basis, preferred_element_type=jnp.float32
        ).astype(jnp.bfloat16)
        parts = [turned[0]] + [swapped(turned[mask], group, mask) for mask in range(1, group)]
        stacked = jnp.stack(parts)
        turned_tokens = jnp.concatenate(
            [
                lax.dynamic_index_in_dim(stacked, place ^ head, axis=0, keepdims=False)
                for head in range(group)
            ],
            axis=1,
        )

    with jax.named_scope("influence"):
        score = jnp.sum(mapped * turned_tokens.astype(jnp.float32), axis=1)
        return lax.psum(score, "head")


def solution(mesh):
    return jax.shard_map(
        on_device,
        mesh=mesh,
        in_specs=(
            P("seq", "head"),
            P("seq", "head"),
            P("seq", "head"),
            P("seq", "head"),
            P("seq", "head"),
            P("head", None, None),
            P("head", None),
            P(None, "head"),
            P(None, "head"),
        ),
        out_specs=P("seq"),
        check_vma=False,
    )
```

```python
import math

import jax
import jax.numpy as jnp
from jax import lax
from jax.experimental import pallas as pl
from jax.experimental.pallas import tpu as pltpu
from jax.sharding import PartitionSpec as P

WINDOW = 4096
SCORE_SCALE = 1.0 / 12.0
SOFT_CAP = 50.0
DAMP_FACTOR = 0.1
LOG2E = math.log2(math.e)
MESH = pl.DeviceIdType.MESH


def shifted(value, by):
    size = lax.axis_size("seq")
    pairs = [(i, i + by) for i in range(size) if 0 <= i + by < size]
    return lax.ppermute(value, "seq", pairs)


def swapped(value, group, mask):
    size = lax.axis_size("seq")
    pairs = [(i, (i // group) * group + ((i % group) ^ mask)) for i in range(size)]
    return lax.ppermute(value, "seq", pairs)


def attend_kernel(key_span, query_ref, adjoint_ref, key_ref, rows_ref, basis_ref, out_ref, map_out, scratch):
    weights, total_ref, sum_ref = scratch[:3]
    if rows_ref is not None:
        leave_ref, come_ref, turned_ref, line_send, line_recv, spread_send, spread_recv = scratch[3:10]
        back_send, back_recv, turn_send, turn_recv = scratch[10:]
    block = pl.program_id(0)
    member = pl.program_id(1)
    depth, group, rows, width = key_ref.shape
    me = lax.axis_index("seq")
    place = me % group
    first = me - place
    step_rows = min(rows, 256)

    line = me // group
    turn = 2 * block + member

    def block_copy(index, seq, send_sem, recv_sem):
        view = map_out.at[index]
        return pltpu.make_async_remote_copy(
            src_ref=view,
            dst_ref=view,
            send_sem=send_sem,
            recv_sem=recv_sem,
            device_id={"seq": seq},
            device_id_type=MESH,
        )

    def along(stage, way, index):
        other = (line + (1 if way == 0 else lines - 1)) % lines
        return block_copy(
            index * group + place,
            other * group + place,
            line_send.at[way, stage],
            line_recv.at[way, stage],
        )

    def hop(stage, way):
        if way == 0:
            going, coming = line - stage, line - stage - 1
            return (going >= 0) & (line + 1 < lines), going, coming >= 0, coming
        going, coming = line + stage, line + stage + 1
        return (going < lines) & (line >= 1), going, coming < lines, coming

    def beside(owner, mask):
        return block_copy(
            owner * group + place,
            first + (place ^ mask),
            spread_send.at[owner, mask],
            spread_recv.at[owner, mask],
        )

    def arrival(owner, mask):
        return block_copy(
            owner * group + (place ^ mask),
            first + (place ^ mask),
            spread_send.at[owner, mask],
            spread_recv.at[owner, mask],
        )

    def forward(owner):
        came = 1 + owner % 2
        return block_copy(
            owner * group + (place ^ came),
            first + (place ^ (3 - came)),
            spread_send.at[owner, 3],
            spread_recv.at[owner, 3],
        )

    if rows_ref is not None:
        lines = map_out.shape[0] // group

        def start_hops(stage):
            for way in (0, 1):
                sends, going, unused, unused_too = hop(stage, way)

                @pl.when(sends)
                def start(way=way, going=going):
                    along(stage, way, going).start()

        def await_hops(stage):
            for way in (0, 1):
                unused, unused_too, receives, coming = hop(stage, way)

                @pl.when(receives)
                def wait(way=way, coming=coming):
                    along(stage, way, coming).wait_recv()

        @pl.when(turn == 0)
        def start_map():
            barrier = pltpu.get_barrier_semaphore()
            for mask in range(1, group):
                pl.semaphore_signal(
                    barrier, inc=1, device_id={"seq": first + (place ^ mask)}, device_id_type=MESH
                )
            for step in (1, lines - 1):
                pl.semaphore_signal(
                    barrier,
                    inc=1,
                    device_id={"seq": ((line + step) % lines) * group + place},
                    device_id_type=MESH,
                )
            here = pltpu.make_async_copy(rows_ref, map_out.at[me], line_recv.at[0, lines - 1])
            here.start()
            here.wait()
            pl.semaphore_wait(barrier, group + 1)
            start_hops(0)

        for stage in range(1, lines):

            @pl.when(turn == stage)
            def next_hop(stage=stage):
                await_hops(stage - 1)
                if stage < lines - 1:
                    start_hops(stage)
                else:
                    for owner in range(lines):
                        for mask in range(1, group):
                            if mask != 3:
                                beside(owner, mask).start()

        if group == 4:

            @pl.when(turn == lines + 2)
            def forward_map():
                for owner in range(lines):
                    arrival(owner, 1 + owner % 2).wait_recv()
                    forward(owner).start()

    @pl.when((block == 0) & (member == 0))
    def clear():
        sum_ref[...] = jnp.zeros_like(sum_ref)

    def where_is(offset):
        line = (depth - 1) * group + block - offset
        back = depth - 1 - line // group
        return back, (line % group) ^ place

    own_slot = block ^ place
    query = query_ref[own_slot]
    total_ref[...] = jnp.zeros_like(total_ref)
    for offset in range(key_span + 1):

        @pl.when(first + block >= offset)
        def score(offset=offset):
            back, slot = where_is(offset)
            for start in range(0, rows, step_rows):
                keys = key_ref[back, slot, pl.ds(start, step_rows), :]
                raw = lax.dot_general(
                    keys, query, (((1,), (1,)), ((), ())), preferred_element_type=jnp.float32
                )
                turned = jnp.tanh(raw * (SCORE_SCALE / SOFT_CAP))
                weight = jnp.exp2(turned * (SOFT_CAP * LOG2E))
                if offset == 0 or offset == key_span:
                    key_pos = start + lax.broadcasted_iota(jnp.int32, weight.shape, 0)
                    query_pos = lax.broadcasted_iota(jnp.int32, weight.shape, 1)
                    keep = key_pos <= query_pos if offset == 0 else key_pos > query_pos
                    weight = jnp.where(keep, weight, 0.0)
                total_ref[...] += jnp.sum(weight.reshape(-1, 8, rows), axis=0)
                weights[offset, pl.ds(start, step_rows), :] = weight.astype(jnp.bfloat16)

    total = jnp.sum(total_ref[...], axis=0, keepdims=True)
    inverse = jnp.broadcast_to(1.0 / total, (width, rows)).T
    scaled = (adjoint_ref[own_slot].astype(jnp.float32) * inverse).astype(jnp.bfloat16)
    for offset in range(key_span + 1):

        @pl.when(first + block >= offset)
        def spread(offset=offset):
            back, slot = where_is(offset)
            sum_ref[back, slot] += jnp.dot(
                weights[offset], scaled, preferred_element_type=jnp.float32
            )

    @pl.when((block == group - 1) & (member == 1))
    def finish():
        if rows_ref is None:
            out_ref[...] = sum_ref[...].astype(out_ref.dtype)
        else:
            span = depth - 1
            size = map_out.shape[0]

            def returned(back):
                return pltpu.make_async_remote_copy(
                    src_ref=leave_ref.at[back - 1],
                    dst_ref=come_ref.at[back - 1],
                    send_sem=back_send.at[back],
                    recv_sem=back_recv.at[back],
                    device_id={"seq": (me + size - group) % size},
                    device_id_type=MESH,
                )

            def absorb(back):
                @pl.when((me + group < size) & (me >= (back - 1) * group))
                def add():
                    returned(back).wait_recv()
                    sum_ref[back - 1] += come_ref[back - 1].astype(jnp.float32)

            for back in range(span, 0, -1):
                if back < span:
                    absorb(back + 1)
                leave_ref[back - 1] = sum_ref[back].astype(leave_ref.dtype)

                @pl.when(me >= back * group)
                def leave(back=back):
                    returned(back).start()

            absorb(1)
            value = sum_ref[0].astype(jnp.bfloat16).reshape(group * rows, width)
            turned = jnp.dot(value, basis_ref[place], preferred_element_type=jnp.float32)
            turned_ref[...] = turned.astype(jnp.bfloat16).reshape(group, rows, width)

            def dealt(mask, head):
                return pltpu.make_async_remote_copy(
                    src_ref=turned_ref.at[mask],
                    dst_ref=out_ref.at[head],
                    send_sem=turn_send.at[mask],
                    recv_sem=turn_recv.at[mask],
                    device_id={"seq": first + (place ^ mask)},
                    device_id_type=MESH,
                )

            own = pltpu.make_async_copy(turned_ref.at[0], out_ref.at[place], turn_recv.at[0])
            own.start()
            for mask in range(1, group):
                dealt(mask, place).start()
            own.wait()
            for mask in range(1, group):
                dealt(mask, place ^ mask).wait_recv()
                dealt(mask, place).wait_send()
            for back in range(span, 0, -1):

                @pl.when(me >= back * group)
                def left(back=back):
                    returned(back).wait_send()

            for stage in range(lines - 1):
                for way in (0, 1):
                    sends, going, unused, unused_too = hop(stage, way)

                    @pl.when(sends)
                    def sent(stage=stage, way=way, going=going):
                        along(stage, way, going).wait_send()

            for owner in range(lines):
                for mask in range(1, group):
                    if group != 4 or mask != 1 + owner % 2:
                        arrival(owner, mask).wait_recv()
                    (forward(owner) if mask == 3 else beside(owner, mask)).wait_send()


def attend(query, adjoint, keys, map_rows, basis_grad, size, key_span):
    depth, group, rows, width = keys.shape
    spreads = map_rows is not None

    def body(*refs):
        query_ref, adjoint_ref, key_ref = refs[:3]
        if spreads:
            rows_ref, basis_ref, out_ref, map_out = refs[3:7]
            scratch = refs[7:]
        else:
            rows_ref, basis_ref, out_ref, map_out = None, None, refs[3], None
            scratch = refs[4:]
        attend_kernel(
            key_span, query_ref, adjoint_ref, key_ref, rows_ref, basis_ref, out_ref, map_out, scratch
        )

    tiles = 2 * group * (key_span + 1) * rows * rows
    whole = pl.BlockSpec((group, rows, width), lambda b, m: (0, 0, m))
    every = pl.BlockSpec((depth, group, rows, width), lambda b, m: (0, 0, 0, 0))
    anywhere = pl.BlockSpec(memory_space=pl.ANY)
    args, in_specs = (query, adjoint, keys), [whole, whole, every]
    outs = [jax.ShapeDtypeStruct((depth, group, rows, width), jnp.bfloat16)]
    out_specs = [every]
    scratch = [
        pltpu.VMEM((key_span + 1, rows, rows), jnp.bfloat16),
        pltpu.VMEM((8, rows), jnp.float32),
        pltpu.VMEM((depth, group, rows, width), jnp.float32),
    ]
    params = {}
    if spreads:
        lines = size // group
        args = args + (map_rows, basis_grad)
        in_specs = in_specs + [anywhere, pl.BlockSpec(basis_grad.shape, lambda b, m: (0, 0, 0))]
        outs = [jax.ShapeDtypeStruct((group, rows, width), jnp.bfloat16)]
        out_specs = [anywhere]
        passing = pltpu.VMEM((depth - 1, group, rows, width), jnp.bfloat16)
        scratch = scratch + [passing, passing, pltpu.VMEM((group, rows, width), jnp.bfloat16)]
        outs.append(jax.ShapeDtypeStruct((size,) + map_rows.shape, map_rows.dtype))
        out_specs.append(anywhere)
        scratch = scratch + [pltpu.SemaphoreType.DMA((2, lines))] * 2
        scratch = scratch + [pltpu.SemaphoreType.DMA((lines, group))] * 2
        scratch = scratch + [pltpu.SemaphoreType.DMA((depth,))] * 2
        scratch = scratch + [pltpu.SemaphoreType.DMA((group,))] * 2
        params = {"collective_id": 1, "has_side_effects": True}
    got = pl.pallas_call(
        body,
        grid=(group, 2),
        in_specs=in_specs,
        out_specs=out_specs,
        out_shape=outs,
        scratch_shapes=scratch,
        compiler_params=pltpu.CompilerParams(vmem_limit_bytes=58 * 1024 * 1024, **params),
        cost_estimate=pl.CostEstimate(
            flops=4 * tiles * width, bytes_accessed=8 * keys.size, transcendentals=2 * tiles
        ),
    )(*args)
    return got if spreads else list(got) + [None]


def exchange_kernel(group, span, reduces, *refs):
    if reduces:
        part_ref, basis_any, eigen_any, turned_ref = refs[:4]
        refs = refs[4:]
    query_ref, adjoint_ref, key_ref, query_out, adjoint_out, key_out = refs[:6]
    refs = refs[6:]
    if reduces:
        map_rows, refs = refs[0], refs[1:]
    deal_send, deal_recv, far_send, far_recv = refs[:4]
    if reduces:
        got_ref, rotated_ref, eigen_sum, map_sum, map_got = refs[4:9]
        part_send, part_recv, sum_send, sum_recv = refs[9:13]
        pair_send, pair_recv, load_sem, basis_ref, eigen_ref = refs[13:]
    me = lax.axis_index("seq")
    size = lax.axis_size("seq")
    place = me % group
    base = me - place
    width = key_ref.shape[1] // group

    barrier = pltpu.get_barrier_semaphore()
    for step in range(1, size):
        pl.semaphore_signal(
            barrier, inc=1, device_id={"seq": (me + step) % size}, device_id_type=MESH
        )
    if reduces:
        head = lax.axis_index("head")
        pl.semaphore_signal(
            barrier, inc=1, device_id={"head": 1 - head}, device_id_type=MESH
        )
        pl.semaphore_wait(barrier, size)
    else:
        pl.semaphore_wait(barrier, size - 1)

    def deal(kind, mask):
        source, target, columns = (
            (key_ref, key_out.at[0], width),
            (query_ref, query_out, 2 * width),
            (adjoint_ref, adjoint_out, 2 * width),
        )[kind]
        other = place ^ mask
        view = source.at[:, pl.ds(pl.multiple_of(other * columns, 128), columns)]
        if mask == 0:
            return pltpu.make_async_copy(view, target.at[0], deal_recv.at[kind, 0])
        return pltpu.make_async_remote_copy(
            src_ref=view,
            dst_ref=target.at[mask],
            send_sem=deal_send.at[kind, mask],
            recv_sem=deal_recv.at[kind, mask],
            device_id={"seq": base + other},
            device_id_type=MESH,
        )

    def far(back):
        return pltpu.make_async_remote_copy(
            src_ref=key_out.at[back - 1],
            dst_ref=key_out.at[back],
            send_sem=far_send.at[back],
            recv_sem=far_recv.at[back],
            device_id={"seq": (me + group) % size},
            device_id_type=MESH,
        )

    def sends(back):
        return (me + group < size) & (me >= (back - 1) * group)

    def part(step):
        peer = (me + step) % size
        return pltpu.make_async_remote_copy(
            src_ref=part_ref.at[peer],
            dst_ref=got_ref.at[me],
            send_sem=part_send.at[step],
            recv_sem=part_recv.at[step],
            device_id={"seq": peer},
            device_id_type=MESH,
        )

    def part_arrival(step):
        peer = (me + size - step) % size
        return pltpu.make_async_remote_copy(
            src_ref=part_ref.at[me],
            dst_ref=got_ref.at[peer],
            send_sem=part_send.at[step],
            recv_sem=part_recv.at[step],
            device_id={"seq": peer},
            device_id_type=MESH,
        )

    def whole(step, source, peer):
        depth = part_ref.shape[1]
        view = rotated_ref.at[pl.ds(pl.multiple_of(source * depth, 16), depth), :]
        return pltpu.make_async_remote_copy(
            src_ref=view,
            dst_ref=view,
            send_sem=sum_send.at[step],
            recv_sem=sum_recv.at[step],
            device_id={"seq": peer},
            device_id_type=MESH,
        )

    def pair(which, source, target):
        return pltpu.make_async_remote_copy(
            src_ref=source,
            dst_ref=target,
            send_sem=pair_send.at[which],
            recv_sem=pair_recv.at[which],
            device_id={"head": 1 - head},
            device_id_type=MESH,
        )

    keys = [deal(0, mask) for mask in range(group)]
    for copy in keys:
        copy.start()
    if reduces:
        parts = [part(step) for step in range(1, size)]
        for copy in parts:
            copy.start()
        features, outputs = eigen_ref.shape
        chunk = 256 if features % 256 == 0 else 128
        loads = [
            pltpu.make_async_copy(eigen_any, eigen_ref, load_sem.at[0]),
            pltpu.make_async_copy(basis_any, basis_ref, load_sem.at[1]),
        ]
        for copy in loads:
            copy.start()

        def add_eigen(index, total):
            some = eigen_ref[pl.ds(pl.multiple_of(index * chunk, chunk), chunk), :]
            return total + jnp.sum(some.astype(jnp.float32).reshape(-1, 8, outputs), axis=0)

        got_ref[me] = part_ref[me]
        for step in range(1, size):
            part_arrival(step).wait_recv()
        total = jnp.sum(got_ref[...].astype(jnp.float32), axis=0)
        depth = part_ref.shape[1]
        rotated_ref[pl.ds(pl.multiple_of(me * depth, 16), depth), :] = total.astype(
            rotated_ref.dtype
        )
        sums = [whole(step, me, (me + step) % size) for step in range(1, size)]
        for copy in sums:
            copy.start()
        for copy in parts:
            copy.wait_send()
        loads[0].wait()
        eigen_part = lax.fori_loop(
            0, features // chunk, add_eigen, jnp.zeros((8, outputs), jnp.float32)
        )
        eigen_part = jnp.sum(eigen_part, axis=0, keepdims=True)
        eigen_part = jnp.sum(eigen_part, axis=1, keepdims=True)
        eigen_sum[0] = jnp.broadcast_to(eigen_part, (8, 128))
        eigen_copy = pair(0, eigen_sum.at[0], eigen_sum.at[1])
        eigen_copy.start()
        for step in range(1, size):
            whole(step, (me + size - step) % size, (me + step) % size).wait_recv()
        for copy in sums:
            copy.wait_send()

    keys[0].wait()
    for copy in keys[1:]:
        copy.wait_recv()
    @pl.when(sends(1))
    def send():
        far(1).start()

    wide = [deal(kind, mask) for kind in (1, 2) for mask in range(group)]
    for mask in range(group):
        for kind in (1, 2):
            wide[(kind - 1) * group + mask].start()

    if reduces:
        eigen_copy.wait()
        loads[1].wait()
        damping = (eigen_sum[0, 0:1, 0:1] + eigen_sum[1, 0:1, 0:1]) * (
            DAMP_FACTOR / (2 * features * outputs)
        )
        map_sum[...] = jnp.zeros_like(map_sum)

        def add_map(index, unused):
            start = pl.multiple_of(index * chunk, chunk)
            gradient = jnp.dot(
                rotated_ref[pl.ds(start, chunk), :],
                turned_ref[...],
                preferred_element_type=jnp.float32,
            )
            spectrum = eigen_ref[pl.ds(start, chunk), :].astype(jnp.float32) + damping
            scaled = (gradient * (1.0 / turned_ref.shape[0]) / spectrum).astype(jnp.bfloat16)
            map_sum[...] += jnp.dot(
                basis_ref[:, pl.ds(start, chunk)], scaled, preferred_element_type=jnp.float32
            )
            return unused

        lax.fori_loop(0, features // chunk, add_map, 0)
        half = outputs // 2
        own = pl.ds(pl.multiple_of(head * half, 128), half)
        other = pl.ds(pl.multiple_of((1 - head) * half, 128), half)
        map_copy = pair(1, map_sum.at[:, other], map_got)
        map_copy.start()
        map_copy.wait()
        map_rows[...] = (map_sum[:, own] + map_got[...]).astype(jnp.bfloat16)

    for back in range(1, span + 1):

        @pl.when(me >= back * group)
        def arrived(back=back):
            far(back).wait_recv()

        if back < span:

            @pl.when(sends(back + 1))
            def pass_on(back=back):
                far(back + 1).start()

    for back in range(1, span + 1):

        @pl.when(sends(back))
        def sent(back=back):
            far(back).wait_send()

    for copy in keys[1:]:
        copy.wait_send()
    for place_in, copy in enumerate(wide):
        if place_in % group == 0:
            copy.wait()
        else:
            copy.wait_recv()
            copy.wait_send()


def exchange(query_rows, out_adjoint, key_rows, map_inputs, group, span):
    rows, columns = key_rows.shape
    width = columns // group
    reduces = map_inputs is not None
    anywhere = pl.BlockSpec(memory_space=pl.ANY)
    in_vmem = pl.BlockSpec(memory_space=pltpu.VMEM)
    wide = jax.ShapeDtypeStruct((group, rows, 2 * width), jnp.bfloat16)
    outs = [wide, wide, jax.ShapeDtypeStruct((span + 1, group, rows, width), jnp.bfloat16)]
    dma = pltpu.SemaphoreType.DMA
    scratch = [dma((3, group)), dma((3, group)), dma((span + 1,)), dma((span + 1,))]
    args = (query_rows, out_adjoint, key_rows)
    in_specs = [anywhere] * 3
    flops = 0
    if reduces:
        part, basis, eigvals, turned = map_inputs
        size, depth, count = part.shape
        outputs = eigvals.shape[1]
        own_map = (basis.shape[0], outputs // 2)
        args = tuple(map_inputs) + args
        in_specs = [in_vmem, anywhere, anywhere, in_vmem] + in_specs
        outs.append(jax.ShapeDtypeStruct(own_map, jnp.bfloat16))
        scratch = scratch + [
            pltpu.VMEM(part.shape, part.dtype),
            pltpu.VMEM((size * depth, count), part.dtype),
            pltpu.VMEM((2, 8, 128), jnp.float32),
            pltpu.VMEM((basis.shape[0], outputs), jnp.float32),
            pltpu.VMEM(own_map, jnp.float32),
        ]
        scratch = scratch + [dma((size,))] * 4 + [dma((2,))] * 3
        scratch = scratch + [pltpu.VMEM(basis.shape, basis.dtype), pltpu.VMEM(eigvals.shape, eigvals.dtype)]
        flops = 2 * basis.size * outputs

    def body(*refs):
        exchange_kernel(group, span, reduces, *refs)

    got = pl.pallas_call(
        body,
        in_specs=in_specs,
        out_specs=[anywhere] * 3 + [in_vmem] * (len(outs) - 3),
        out_shape=outs,
        scratch_shapes=scratch,
        compiler_params=pltpu.CompilerParams(
            collective_id=0, has_side_effects=True, vmem_limit_bytes=58 * 1024 * 1024
        ),
        cost_estimate=pl.CostEstimate(
            flops=flops, bytes_accessed=16 * key_rows.size, transcendentals=0
        ),
    )(*args)
    return got if reduces else list(got) + [None]


def on_device(
    act, query_rows, key_rows, out_adjoint, basis_input, basis_grad, eigvals, query_act, query_adj
):
    local_rows = act.shape[0]
    group = basis_grad.shape[0]
    width = basis_grad.shape[1]
    key_span = WINDOW // local_rows
    span = key_span // group
    seq_index = lax.axis_index("seq")
    place = seq_index % group

    with jax.named_scope("rotated_part"):
        row_count, column_count = basis_input.shape
        query_count = query_act.shape[0]
        size = lax.axis_size("seq")
        full_query_act = lax.all_gather(query_act, "head", axis=1, tiled=True)
        own_rows = lax.dynamic_slice_in_dim(
            full_query_act, seq_index * row_count, row_count, axis=1
        )
        part = lax.dot_general(
            basis_input, own_rows, (((0,), (1,)), ((), ())), preferred_element_type=jnp.float32
        )
        reduces = column_count % (16 * size) == 0 and lax.axis_size("head") == 2 and group in (2, 4)
        reduces = reduces and size // group + 2 < 2 * group
        if reduces:
            part = part.astype(jnp.bfloat16).reshape(size, column_count // size, query_count)

    with jax.named_scope("turned_query"):
        split_query = query_adj.reshape(query_count, group, width)
        turned_query = jnp.einsum(
            "the,hef->thf", split_query, basis_grad, preferred_element_type=jnp.float32
        )
        turned_query = turned_query.reshape(query_adj.shape).astype(jnp.bfloat16)
        all_turned_query = lax.all_gather(turned_query, "head", axis=1, tiled=True)

    with jax.named_scope("spread_heads"):
        map_inputs = (part, basis_input, eigvals, all_turned_query) if reduces else None
        queries, adjoints, keys, map_rows = exchange(
            query_rows, out_adjoint, key_rows, map_inputs, group, span
        )

    with jax.named_scope("attention"):
        attended, token_map = attend(
            queries, adjoints, keys, map_rows, basis_grad, size, key_span
        )
        if reduces:
            token_map = token_map.reshape(row_count * size, -1)

    if not reduces:
        with jax.named_scope("token_map"):
            rotated_query = lax.psum(part, "seq").astype(jnp.bfloat16)
            query_grad = (
                jnp.dot(rotated_query, all_turned_query, preferred_element_type=jnp.float32)
                / query_count
            )
            eigen_total = lax.psum(jnp.sum(eigvals, dtype=jnp.float32), "head")
            eigen_count = eigvals.shape[0] * lax.axis_size("head") * eigvals.shape[1]
            damping = DAMP_FACTOR * eigen_total / eigen_count
            scaled = (query_grad / (eigvals.astype(jnp.float32) + damping)).astype(jnp.bfloat16)
            map_part = jnp.dot(basis_input, scaled, preferred_element_type=jnp.float32)
            map_rows = lax.psum_scatter(map_part, "head", scatter_dimension=1, tiled=True)
            token_map = lax.all_gather(map_rows.astype(jnp.bfloat16), "seq", axis=0, tiled=True)

    with jax.named_scope("mapped"):
        full_act = lax.all_gather(act, "head", axis=1, tiled=True)
        mapped = jnp.dot(full_act, token_map, preferred_element_type=jnp.float32)

    if reduces:
        heads = [attended[head] for head in range(group)]
    else:
        with jax.named_scope("value_adjoint"):
            carried = shifted(attended[span], -group)
            for back in range(span - 1, 0, -1):
                passed = attended[back].astype(jnp.float32) + carried.astype(jnp.float32)
                carried = shifted(passed.astype(jnp.bfloat16), -group)
            adjoint_sum = attended[0].astype(jnp.float32) + carried.astype(jnp.float32)
            value_adjoint = adjoint_sum.astype(jnp.bfloat16)

        with jax.named_scope("gather_heads"):
            own_basis = lax.dynamic_index_in_dim(basis_grad, place, axis=0, keepdims=False)
            turned = jnp.einsum(
                "gte,ef->gtf", value_adjoint, own_basis, preferred_element_type=jnp.float32
            ).astype(jnp.bfloat16)
            parts = [turned[0]] + [swapped(turned[mask], group, mask) for mask in range(1, group)]
            stacked = jnp.stack(parts)
            heads = [
                lax.dynamic_index_in_dim(stacked, place ^ head, axis=0, keepdims=False)
                for head in range(group)
            ]

    with jax.named_scope("influence"):
        score = jnp.zeros((local_rows,), jnp.float32)
        for head in range(group):
            own_map = mapped[:, head * width : (head + 1) * width]
            score = score + jnp.sum(own_map * heads[head].astype(jnp.float32), axis=1)
        return lax.psum(score, "head")


def solution(mesh):
    return jax.shard_map(
        on_device,
        mesh=mesh,
        in_specs=(
            P("seq", "head"),
            P("seq", "head"),
            P("seq", "head"),
            P("seq", "head"),
            P("seq", "head"),
            P("head", None, None),
            P("head", None),
            P(None, "head"),
            P(None, "head"),
        ),
        out_specs=P("seq"),
        check_vma=False,
    )
```
